32 devices in a mesh: pool: 4 (over y, x), seq: 8 (over z, core).
Axes of the slice: x: 2, y: 2, z: 4, core: 2. Of those that a mesh axis runs over, the one named last changes fastest.
Arguments:
- pool_kv: bfloat16 [16, 1024, 1024], P('pool', 'seq'), may hold values from -4 to 4
- span_home: int32 [12], replicated, may hold values from 0 to 15, as said below
- span_order: int32 [4, 3], P('pool'), may hold values from 0 to 11, as said below
- chosen: int32 [4, 3], P('pool'), may hold values from 0 to 23, as said below
- fresh_q: bfloat16 [4, 384, 6144], P('pool', 'seq'), may hold values from -300 to 300
- fresh_kv: bfloat16 [4, 384, 1024], P('pool', 'seq'), may hold values from -5 to 5
Outputs:
- attended: bfloat16 [4, 384, 6144], P('pool', 'seq')
- decode_kv: bfloat16 [4, 8, 4, 24, 4096], P('pool', 'seq')
The draws below stay inside these ranges and needn't reach their ends.
Inputs may be any that keep to these rules, and one draw needn't show every extreme that they name: `span_home`: all entries differ; home // 4 is the replica of a passage, and the 3 passages r * 3 to r * 3 + 2 of request r lie on different replicas; some replica holds a passage of every request. `span_order`: row r orders the passages r * 3 to r * 3 + 2. `chosen`: each row lists 3 different blocks in rising order; block k holds positions k * 128 to k * 128 + 127.
All inputs are finite; a program needn't handle non-finite values.
Results may differ from the reference program's by a relative error of at most 0.0035.
Values may be sent and summed in bfloat16 or wider, within the bound.
No kernel may reach another device: no remote copies, remote signals or barrier semaphores. Data moves between devices by JAX's collectives and lax.ppermute only.
A program may use at most 192 MiB of HBM per device.

```python
import jax
import jax.numpy as jnp
from jax import lax

HEADS = 48
KV_HEADS = 4
HEAD_DIM = 128
BLOCK = 128
SPANS = 3
GROUP = 12
REQUESTS = 4
SLOTS = 4
SPAN_LEN = 1024
BLOCKS = 24
SELECTED = 3
PICKED_ROWS = 384
RUN = 16
N_POOL = 4
N_SEQ = 8


def draw_span_home(key, part):
    favored = jax.random.randint(jax.random.fold_in(key, 1), (), 0, REQUESTS)
    replicas = jnp.arange(REQUESTS, dtype=jnp.int32)
    raw_score = jax.random.randint(jax.random.fold_in(key, 2), (REQUESTS, REQUESTS), 0, 1024)
    scores = (raw_score + 2048 * (replicas[None, :] == favored).astype(jnp.int32)) * REQUESTS + replicas[None, :]
    ranked = jnp.argsort(-scores, axis=1)
    picked_rep = ranked[:, :SPANS].astype(jnp.int32)
    slot_score = jax.random.randint(jax.random.fold_in(key, 3), (REQUESTS, SLOTS), 0, 1 << 20) * SLOTS + jnp.arange(SLOTS, dtype=jnp.int32)[None, :]
    slot_perm = jnp.argsort(slot_score, axis=1).astype(jnp.int32)
    owners = jnp.broadcast_to(jnp.arange(REQUESTS, dtype=jnp.int32)[:, None], (REQUESTS, SPANS))
    slot_of = slot_perm[picked_rep, owners]
    return (picked_rep * SLOTS + slot_of).reshape(REQUESTS * SPANS).astype(jnp.int32)


def draw_span_order(key, part):
    scores = jax.random.randint(jax.random.fold_in(key, 21), (REQUESTS, SPANS), 0, 1 << 20) * SPANS + jnp.arange(SPANS, dtype=jnp.int32)[None, :]
    ranked = jnp.argsort(scores, axis=1).astype(jnp.int32)
    return (ranked + jnp.arange(REQUESTS, dtype=jnp.int32)[:, None] * SPANS).astype(jnp.int32)


def draw_chosen(key, part):
    scores = jax.random.randint(jax.random.fold_in(key, 31), (REQUESTS, BLOCKS), 0, 1 << 20) * BLOCKS + jnp.arange(BLOCKS, dtype=jnp.int32)[None, :]
    ranked = jnp.argsort(scores, axis=1)[:, :SELECTED]
    return jnp.sort(ranked, axis=1).astype(jnp.int32)


def fresh_pair(key):
    row_total = PICKED_ROWS
    base = jnp.clip(jax.random.normal(jax.random.fold_in(key, 101), (REQUESTS, row_total, KV_HEADS, 2, HEAD_DIM), jnp.float32), -4.0, 4.0)
    query = 3.0 * jnp.clip(jax.random.normal(jax.random.fold_in(key, 102), (REQUESTS, row_total, KV_HEADS, GROUP, HEAD_DIM), jnp.float32), -4.0, 4.0)
    query = jnp.clip(query, -300.0, 300.0).reshape(REQUESTS, row_total, HEADS * HEAD_DIM)
    base = jnp.clip(base, -5.0, 5.0).reshape(REQUESTS, row_total, KV_HEADS * 2 * HEAD_DIM)
    return (query, base)


def draw_fresh_q(key, part):
    return fresh_pair(key)[0].astype(jnp.bfloat16)


def draw_fresh_kv(key, part):
    return fresh_pair(key)[1].astype(jnp.bfloat16)


def block_levels(rng, extent, cuts, low, high):
    factor_of = 1.0
    for position, blocks in cuts:
        heights = jax.random.uniform(jax.random.fold_in(jax.random.fold_in(rng, 6), position), (blocks,), jnp.float32, low / len(cuts), high / len(cuts))
        factor_of = factor_of * jnp.repeat(jnp.exp(heights), extent[position] // blocks).reshape((-1,) + (1,) * (len(extent) - 1 - position))
    return factor_of


def scatter_about(rng, shape, scale, most, cuts=(), kind=jnp.bfloat16):
    entries = scale * jax.random.normal(rng, shape, jnp.float32)
    if cuts:
        entries = entries * block_levels(rng, shape, cuts, -0.22, 0.18)
    return jnp.clip(entries, -most, most).astype(kind)


def setup_inputs(seed: int = 0) -> dict:
    seeds = jax.random.split(jax.random.key(seed), 7)
    return {
        "pool_kv": scatter_about(seeds[0], (N_POOL * SLOTS, SPAN_LEN, KV_HEADS * 2 * HEAD_DIM), 1.0, 4.0, ((0, 4), (1, 8))),
        "span_home": draw_span_home(jax.random.fold_in(seeds[6], 71), 0),
        "span_order": draw_span_order(jax.random.fold_in(seeds[6], 71), 0),
        "chosen": draw_chosen(jax.random.fold_in(seeds[6], 71), 0),
        "fresh_q": draw_fresh_q(jax.random.fold_in(seeds[6], 71), 0),
        "fresh_kv": draw_fresh_kv(jax.random.fold_in(seeds[6], 71), 0),
    }


def attend_request(queries, context, places):
    length = context.shape[0]
    split = context.reshape(length, KV_HEADS, 2, HEAD_DIM).astype(jnp.float32)
    keys = split[:, :, 0]
    values = split[:, :, 1]
    grouped = queries.reshape(SELECTED, BLOCK, KV_HEADS, GROUP, HEAD_DIM)
    spots = places.reshape(SELECTED, BLOCK)
    key_pos = jnp.arange(length, dtype=jnp.int32)

    def one_block(pair):
        block_q, block_pos = pair
        scores = jnp.einsum("tkgd,lkd->kgtl", block_q.astype(jnp.float32), keys) * (HEAD_DIM ** -0.5)
        allowed = key_pos[None, None, None, :] <= block_pos[None, None, :, None]
        scores = jnp.where(allowed, scores, -jnp.inf)
        top = jnp.max(scores, axis=-1, keepdims=True)
        weights = jnp.where(allowed, jnp.exp(scores - top), 0.0)
        total = jnp.sum(weights, axis=-1)
        rounded = lax.optimization_barrier(weights.astype(jnp.bfloat16)).astype(jnp.float32)
        mixed = jnp.einsum("kgtl,lkd->tkgd", rounded, values)
        mixed = mixed / jnp.transpose(total, (2, 0, 1))[..., None]
        return mixed.reshape(BLOCK, HEADS * HEAD_DIM).astype(jnp.bfloat16)

    return lax.map(one_block, (grouped, spots)).reshape(SELECTED * BLOCK, HEADS * HEAD_DIM)


def reference(pool_kv, span_home, span_order, chosen, fresh_q, fresh_kv):
    kv_width = pool_kv.shape[-1]
    attended_all = []
    contexts = []
    for request in range(REQUESTS):
        slot_list = span_home[span_order[request]].astype(jnp.int32)
        context = pool_kv[slot_list].reshape(SPANS * SPAN_LEN, kv_width)
        places = (chosen[request][:, None] * BLOCK + jnp.arange(BLOCK, dtype=jnp.int32)[None, :]).reshape(-1).astype(jnp.int32)
        context = context.at[places].set(fresh_kv[request])
        contexts.append(context)
        attended_all.append(attend_request(fresh_q[request], context, places))
    attended = jnp.stack(attended_all)
    stacked = jnp.stack(contexts).reshape(REQUESTS, BLOCKS, N_SEQ, RUN, KV_HEADS, 2 * HEAD_DIM)
    decode_kv = stacked.transpose(4, 2, 0, 1, 3, 5).reshape(KV_HEADS, N_SEQ, REQUESTS, BLOCKS, RUN * 2 * HEAD_DIM)
    return attended, decode_kv
```

```python
import functools
import math

import jax
import jax.numpy as jnp
from jax import lax
from jax.experimental import pallas as pl
from jax.experimental.pallas import tpu as pltpu
from jax.sharding import Mesh, PartitionSpec as P

KV_HEADS = 4
HEAD_DIM = 128
LOW = -1e30

SMEM = pl.BlockSpec(memory_space=pltpu.SMEM)
VMEM = pl.BlockSpec(memory_space=pltpu.VMEM)
ANY = pl.BlockSpec(memory_space=pl.ANY)
PARAMS = pltpu.CompilerParams(vmem_limit_bytes=40 * 1024 * 1024)


def pack_kernel(slots, spans, ids, home, pool_kv, fresh_q, fresh_kv, *rest):
    sems = rest[-1]
    pool_count, heads = sems.shape[1], KV_HEADS
    to_pool, to_head = rest[:pool_count], rest[pool_count : pool_count + heads]
    me, head = ids[0], ids[2]
    q_width = fresh_q.shape[2] // heads
    kv_width = fresh_kv.shape[2] // heads
    copies = []
    for d in range(pool_count):
        request = me ^ d
        slot = jnp.int32(0)
        for t in range(spans):
            at = home[request * spans + t]
            slot = jnp.where(at // slots == me, at % slots, slot)
        copies.append(pltpu.make_async_copy(pool_kv.at[slot], to_pool[d], sems.at[0, d]))
        copies[-1].start()
    for d in range(heads):
        other = head ^ d
        q_at = pl.ds(pl.multiple_of(other * q_width, HEAD_DIM), q_width)
        kv_at = pl.ds(pl.multiple_of(other * kv_width, HEAD_DIM), kv_width)
        copies.append(
            pltpu.make_async_copy(fresh_q.at[0, :, q_at], to_head[d].at[:, pl.ds(0, q_width)], sems.at[1, d])
        )
        copies[-1].start()
        copies.append(
            pltpu.make_async_copy(fresh_kv.at[0, :, kv_at], to_head[d].at[:, pl.ds(q_width, kv_width)], sems.at[2, d])
        )
        copies[-1].start()
    for copy in copies:
        copy.wait()


def choose_kernel(slots, ids, home, order, *rest):
    sems = rest[-1]
    spans, heads = sems.shape
    pool_count = len(rest) - 1 - heads
    arrived, out = rest[:pool_count], rest[pool_count : pool_count + heads]
    me, head = ids[0], ids[2]
    width = out[0].shape[2]
    for start in (True, False):
        for j in range(spans):
            source = (home[order[0, j]] // slots) ^ me
            for d in range(heads):
                at = pl.ds(pl.multiple_of((head ^ d) * width, HEAD_DIM), width)
                if start:
                    for p in range(pool_count):

                        @pl.when(source == p)
                        def _(p=p):
                            pltpu.make_async_copy(arrived[p].at[:, at], out[d].at[j], sems.at[j, d]).start()

                else:
                    pltpu.make_async_copy(arrived[0].at[:, at], out[d].at[j], sems.at[j, d]).wait()


def patch_into(dest, at, source, chosen, fresh, message, seq_count):
    spans, block, _ = message.shape
    for j in range(spans):
        dest[pl.ds((at * spans + j) * block, block), :] = message[j]
    for i in range(chosen.shape[1]):
        picked = chosen[0, i]

        @pl.when(picked % seq_count == source)
        def _():
            row = pl.multiple_of((at * spans + picked // seq_count) * block, block)
            dest[pl.ds(row, block), :] = fresh[pl.ds(i * block, block), :]


def attend_kernel(ks, first, last, seq_count, rows, ids, chosen, q, fresh, *rest):
    n = len(ks)
    messages, rest = rest[:n], rest[n:]
    spans, block, _ = messages[0].shape
    quad_rows = q.shape[0]
    group = (q.shape[1] - 2 * HEAD_DIM) // HEAD_DIM
    if not first:
        (acc_in, ml_in), rest = rest[:2], rest[2:]
    outs, (kv, bias) = rest[:-2], rest[-2:]
    me = ids[1] * KV_HEADS + ids[2]
    for at, k in enumerate(ks):
        patch_into(kv, at, me ^ k, chosen, fresh, messages[at], seq_count)

    local = lax.broadcasted_iota(jnp.int32, (quad_rows, 1), 0)
    part = local // rows
    listed = (ids[1] * KV_HEADS + (ids[2] ^ part)) * rows + local % rows
    which = listed // block
    place = jnp.zeros((quad_rows, 1), jnp.int32)
    for i in range(chosen.shape[1]):
        place = jnp.where(which == i, chosen[0, i] * block, place)
    place = place + listed % block
    for at, k in enumerate(ks):
        for j in range(spans):
            key = (j * seq_count + (me ^ k)) * block + lax.broadcasted_iota(jnp.int32, (quad_rows, block), 1)
            bias[:, pl.ds((at * spans + j) * block, block)] = jnp.where(key <= place, 0.0, LOW)

    scale = math.log2(math.e) / math.sqrt(HEAD_DIM)
    lane = lax.broadcasted_iota(jnp.int32, (quad_rows, HEAD_DIM), 1)

    def one_head(h, carry):
        cols = pl.ds(pl.multiple_of(h * HEAD_DIM, HEAD_DIM), HEAD_DIM)
        keys, values = kv[:, :HEAD_DIM], kv[:, HEAD_DIM:]
        s = lax.dot_general(q[:, cols], keys, (((1,), (1,)), ((), ())), preferred_element_type=jnp.float32)
        s = s * scale + bias[...]
        top = jnp.max(s, axis=1, keepdims=True)
        if not first:
            top_in = ml_in[h][:, :1]
            top = jnp.maximum(top, top_in)
        p = jnp.exp2(s - top)
        total = jnp.sum(p, axis=1, keepdims=True)
        acc = jnp.dot(p.astype(jnp.bfloat16), values, preferred_element_type=jnp.float32)
        if not first:
            factor = jnp.exp2(top_in - top)
            total = total + factor * ml_in[h][:, HEAD_DIM // 2 : HEAD_DIM // 2 + 1]
            acc = acc + factor * acc_in[h]
        if last:
            done = acc / total
            for d, out in enumerate(outs):
                out[:, cols] = done[d * rows : (d + 1) * rows].astype(jnp.bfloat16)
        else:
            outs[0][h] = acc
            outs[1][h] = jnp.where(lane < HEAD_DIM // 2, top, total)
        return carry

    lax.fori_loop(0, group, one_head, 0)


def attend(ks, state, last, seq_count, rows, ids, chosen, q, fresh, messages):
    quad_rows, width = q.shape
    group = (width - 2 * HEAD_DIM) // HEAD_DIM
    spans, block, kv_width = messages[0].shape
    keys = len(ks) * spans * block
    if last:
        out_shape = [jax.ShapeDtypeStruct((rows, group * HEAD_DIM), jnp.bfloat16)] * (quad_rows // rows)
    else:
        out_shape = [jax.ShapeDtypeStruct((group, quad_rows, HEAD_DIM), jnp.float32)] * 2
    inputs = [ids, chosen, q, fresh, *messages, *(state or ())]
    return pl.pallas_call(
        functools.partial(attend_kernel, ks, state is None, last, seq_count, rows),
        out_shape=out_shape,
        in_specs=[SMEM, SMEM] + [VMEM] * (len(inputs) - 2),
        out_specs=[VMEM] * len(out_shape),
        scratch_shapes=[pltpu.VMEM((keys, kv_width), jnp.bfloat16), pltpu.VMEM((quad_rows, keys), jnp.float32)],
        compiler_params=PARAMS,
        cost_estimate=pl.CostEstimate(
            flops=4 * group * quad_rows * keys * HEAD_DIM,
            bytes_accessed=4 * quad_rows * width + 2 * keys * kv_width,
            transcendentals=group * quad_rows * keys,
        ),
        name="attend",
    )(*inputs)


def shards(pool_kv, span_home, span_order, chosen, fresh_q, fresh_kv):
    pool_count, quads, heads = (lax.axis_size(a) for a in ("pool", "quad", "head"))
    seq_count = quads * heads
    me, quad, head = (lax.axis_index(a) for a in ("pool", "quad", "head"))
    slots, block, width = pool_kv.shape
    spans = span_order.shape[1]
    rows, q_width = fresh_q.shape[1:]
    kv_width = width // heads
    q_part = q_width // heads
    run = block // seq_count
    ids = jnp.stack([me, quad, head]).astype(jnp.int32)
    seat = quad * heads + head
    bf16 = jnp.bfloat16

    packed = pl.pallas_call(
        functools.partial(pack_kernel, slots, spans),
        out_shape=[jax.ShapeDtypeStruct((block, width), bf16)] * pool_count
        + [jax.ShapeDtypeStruct((rows, q_part + kv_width), bf16)] * heads,
        in_specs=[SMEM, SMEM, ANY, ANY, ANY],
        out_specs=[ANY] * (pool_count + heads),
        scratch_shapes=[pltpu.SemaphoreType.DMA((3, max(pool_count, heads)))],
        compiler_params=PARAMS,
        name="pack",
    )(ids, span_home, pool_kv, fresh_q, fresh_kv)
    to_pool, to_head = packed[:pool_count], packed[pool_count:]

    def swap(value, axes, count, k):
        return lax.ppermute(value, axes, [(i, i ^ k) for i in range(count)])

    arrived = [to_pool[0]] + [None] * (pool_count - 1)
    for k in reversed(range(1, pool_count)):
        arrived[k] = swap(to_pool[k], "pool", pool_count, k)
    gathered = [to_head[0]] + [swap(to_head[k], "head", heads, k) for k in range(1, heads)]
    q = jnp.concatenate(gathered, axis=0)

    kv_out = pl.pallas_call(
        functools.partial(choose_kernel, slots),
        out_shape=[jax.ShapeDtypeStruct((spans, block, kv_width), bf16)] * heads,
        in_specs=[SMEM, SMEM, SMEM] + [ANY] * pool_count,
        out_specs=[ANY] * heads,
        scratch_shapes=[pltpu.SemaphoreType.DMA((spans, heads))],
        compiler_params=PARAMS,
        name="choose",
    )(ids, span_home, span_order, *arrived)

    seq = ("quad", "head")
    messages = [kv_out[0]] + [None] * (seq_count - 1)
    for k in list(range(heads, seq_count)) + list(range(1, heads)):
        messages[k] = swap(kv_out[k % heads], seq, seq_count, k)

    near = q[:, q_part:]
    parts = [near] + [swap(near, "quad", quads, k) for k in range(1, quads)]
    listed = jnp.stack(parts).reshape(seq_count, rows, kv_width)
    fresh = jnp.take(listed, seat ^ jnp.arange(seq_count), axis=0).reshape(seq_count * rows, kv_width)

    groups = [list(range(heads))] + [[k, k + 1] for k in range(heads, seq_count, 2)]
    state = None
    for ks in groups:
        state = attend(
            ks, state, ks is groups[-1], seq_count, rows, ids, chosen, q, fresh, [messages[k] for k in ks]
        )
    back = [state[0]] + [swap(state[k], "head", heads, k) for k in range(1, heads)]
    attended = jnp.take(jnp.stack(back, axis=1), head ^ jnp.arange(heads), axis=1)
    attended = attended.reshape(1, rows, q_width)

    blocks = jnp.stack(messages, axis=1)
    blocks = jnp.take(blocks, seat ^ jnp.arange(seq_count), axis=1).reshape(spans * seq_count, block, kv_width)
    blocks = blocks.at[chosen[0]].set(fresh.reshape(-1, block, kv_width))
    blocks = blocks.reshape(spans * seq_count, quads, heads, run, kv_width)
    mine = lax.dynamic_index_in_dim(blocks, quad, axis=1, keepdims=False)
    landed = []
    for k in range(pool_count):
        perm = [
            ((r * quads + a) * heads + g, (g * quads + a) * heads + (r ^ k))
            for r in range(pool_count)
            for a in range(quads)
            for g in range(heads)
        ]
        part = lax.dynamic_index_in_dim(mine, me ^ k, axis=1, keepdims=False)
        landed.append(lax.ppermute(part, ("pool", "quad", "head"), perm))
    landed = jnp.take(jnp.stack(landed), head ^ jnp.arange(pool_count), axis=0)
    decoded = landed.reshape(1, 1, pool_count, spans * seq_count, run * kv_width)
    return (attended, decoded)


def solution(mesh):
    pool_count, seq_count = mesh.shape["pool"], mesh.shape["seq"]
    fine = Mesh(mesh.devices.reshape(pool_count, seq_count // KV_HEADS, KV_HEADS), ("pool", "quad", "head"))
    seq = ("quad", "head")
    in_specs = (
        P("pool", seq, None),
        P(),
        P("pool", None),
        P("pool", None),
        P("pool", seq, None),
        P("pool", seq, None),
    )
    out_specs = (P("pool", seq, None), P("pool", seq, None, None, None))
    return jax.shard_map(shards, mesh=fine, in_specs=in_specs, out_specs=out_specs, check_vma=False)
```

```python
import functools
import math

import jax
import jax.numpy as jnp
from jax import lax
from jax.experimental import pallas as pl
from jax.experimental.pallas import tpu as pltpu
from jax.sharding import Mesh, PartitionSpec as P

KV_HEADS = 4
HEAD_DIM = 128
LOW = -1e30
BF16 = jnp.bfloat16
F32 = jnp.float32

SMEM = pl.BlockSpec(memory_space=pltpu.SMEM)
VMEM = pl.BlockSpec(memory_space=pltpu.VMEM)
ANY = pl.BlockSpec(memory_space=pl.ANY)
HBM = pl.BlockSpec(memory_space=pltpu.HBM)
PARAMS = pltpu.CompilerParams(vmem_limit_bytes=40 * 1024 * 1024)


def pack_kernel(slots, spans, ids, home, pool_kv, fresh_q, fresh_kv, *rest):
    sems = rest[-1]
    pool_count, heads = (len(rest) - 1 - KV_HEADS) // 2, KV_HEADS
    to_pool, to_head = rest[: 2 * pool_count], rest[2 * pool_count : -1]
    me, head = ids[0], ids[2]
    half = pool_kv.shape[2] // 2
    q_width = fresh_q.shape[2] // heads
    kv_width = fresh_kv.shape[2] // heads
    copies = []
    for d in range(pool_count):
        request = me ^ d
        slot = jnp.int32(0)
        for t in range(spans):
            at = home[request * spans + t]
            slot = jnp.where(at // slots == me, at % slots, slot)
        for c in range(2):
            at = pl.ds(pl.multiple_of(((head // (heads // 2)) ^ c) * half, HEAD_DIM), half)
            copies.append(
                pltpu.make_async_copy(
                    pool_kv.at[slot, :, at], to_pool[c * pool_count + d], sems.at[0, c * pool_count + d]
                )
            )
            copies[-1].start()
    for d in range(heads):
        other = head ^ d
        q_at = pl.ds(pl.multiple_of(other * q_width, HEAD_DIM), q_width)
        kv_at = pl.ds(pl.multiple_of(other * kv_width, HEAD_DIM), kv_width)
        copies.append(
            pltpu.make_async_copy(fresh_q.at[0, :, q_at], to_head[d].at[:, pl.ds(0, q_width)], sems.at[1, d])
        )
        copies[-1].start()
        copies.append(
            pltpu.make_async_copy(fresh_kv.at[0, :, kv_at], to_head[d].at[:, pl.ds(q_width, kv_width)], sems.at[2, d])
        )
        copies[-1].start()
    for copy in copies:
        copy.wait()


def choose_kernel(slots, ids, home, order, *rest):
    sems = rest[-1]
    spans, heads = sems.shape
    arrived, out = rest[: -1 - heads], rest[-1 - heads : -1]
    me, head = ids[0], ids[2]
    width = out[0].shape[2]
    for start in (True, False):
        for j in range(spans):
            source = (home[order[0, j]] // slots) ^ me
            for d in range(heads):
                at = pl.ds(pl.multiple_of(((head % heads) ^ d) * width, HEAD_DIM), width)
                if start:
                    for p in range(len(arrived)):

                        @pl.when(source == p)
                        def _(p=p):
                            pltpu.make_async_copy(arrived[p].at[:, at], out[d].at[j], sems.at[j, d]).start()

                else:
                    pltpu.make_async_copy(arrived[0].at[:, at], out[d].at[j], sems.at[j, d]).wait()


def attend_kernel(ks, first, last, seq_count, rows, stacked, ids, chosen, q, fresh, *rest):
    messages, rest = rest[: len(ks)], rest[len(ks) :]
    spans, block, _ = messages[0].shape
    quad_rows = q.shape[0]
    group = (q.shape[1] - 2 * HEAD_DIM) // HEAD_DIM
    if not first:
        (acc_in, top_in, total_in), rest = rest[:3], rest[3:]
    outs, (keys, values, bias) = rest[:-3], rest[-3:]
    count = keys.shape[0]
    me = ids[1] * KV_HEADS + ids[2]

    values[:, HEAD_DIM:] = jnp.ones((count, HEAD_DIM), BF16)
    for at, k in enumerate(ks):
        for j in range(spans):
            row = pl.ds((at * spans + j) * block, block)
            keys[row, :] = messages[at][j, :, :HEAD_DIM]
            values[row, :HEAD_DIM] = messages[at][j, :, HEAD_DIM:]
        for i in range(chosen.shape[1]):
            picked = chosen[0, i]

            @pl.when(picked % seq_count == me ^ k)
            def _():
                row = pl.ds(pl.multiple_of((at * spans + picked // seq_count) * block, block), block)
                keys[row, :] = fresh[pl.ds(i * block, block), :HEAD_DIM]
                values[row, :HEAD_DIM] = fresh[pl.ds(i * block, block), HEAD_DIM:]

    local = lax.broadcasted_iota(jnp.int32, (quad_rows, 1), 0)
    listed = (ids[1] * KV_HEADS + (ids[2] ^ (local // rows))) * rows + local % rows
    which = listed // block
    place = jnp.zeros((quad_rows, 1), jnp.int32)
    for i in range(chosen.shape[1]):
        place = jnp.where(which == i, chosen[0, i] * block, place)
    place = place + listed % block
    for at, k in enumerate(ks):
        for j in range(spans):
            key = (j * seq_count + (me ^ k)) * block + lax.broadcasted_iota(jnp.int32, (quad_rows, block), 1)
            bias[:, pl.ds((at * spans + j) * block, block)] = jnp.where(key <= place, 0.0, LOW)

    scale = math.log2(math.e) / math.sqrt(HEAD_DIM)
    wide = stacked * quad_rows
    for h in range(0, group, stacked):
        cols = [pl.ds((h + i) * HEAD_DIM, HEAD_DIM) for i in range(stacked)]
        query = jnp.concatenate([q[:, c] for c in cols], axis=0)
        s = lax.dot_general(query, keys[...], (((1,), (1,)), ((), ())), preferred_element_type=F32)
        s = (s.reshape(stacked, quad_rows, count) * scale + bias[...][None]).reshape(wide, count)
        top = jnp.broadcast_to(jnp.max(s, axis=1, keepdims=True), (wide, HEAD_DIM))
        if not first:
            before = top_in[h // stacked]
            top = jnp.maximum(top, before)
        p = jnp.exp2(s - jnp.concatenate([top] * (count // HEAD_DIM), axis=1))
        both = jnp.dot(p.astype(BF16), values[...], preferred_element_type=F32)
        acc, total = both[:, :HEAD_DIM], both[:, HEAD_DIM:]
        if not first:
            factor = jnp.exp2(before - top)
            acc = acc + factor * acc_in[h // stacked]
            total = total + factor * total_in[h // stacked]
        if last:
            done = acc / total
            for i in range(stacked):
                for d, out in enumerate(outs):
                    at = i * quad_rows + d * rows
                    out[:, cols[i]] = done[at : at + rows].astype(BF16)
        else:
            outs[0][h // stacked] = acc
            outs[1][h // stacked] = top
            outs[2][h // stacked] = total


def attend(ks, state, last, seq_count, rows, ids, chosen, q, fresh, messages):
    quad_rows, width = q.shape
    group = (width - 2 * HEAD_DIM) // HEAD_DIM
    spans, block, kv_width = messages[0].shape
    keys = len(ks) * spans * block
    stacked = 2 - group % 2
    if last:
        out_shape = [jax.ShapeDtypeStruct((rows, group * HEAD_DIM), BF16)] * (quad_rows // rows)
    else:
        out_shape = [jax.ShapeDtypeStruct((group // stacked, stacked * quad_rows, HEAD_DIM), F32)] * 3
    inputs = [ids, chosen, q, fresh, *messages, *(state or ())]
    return pl.pallas_call(
        functools.partial(attend_kernel, ks, state is None, last, seq_count, rows, stacked),
        out_shape=out_shape,
        in_specs=[SMEM, SMEM] + [VMEM] * (len(inputs) - 2),
        out_specs=[VMEM] * len(out_shape),
        scratch_shapes=[
            pltpu.VMEM((keys, HEAD_DIM), BF16),
            pltpu.VMEM((keys, 2 * HEAD_DIM), BF16),
            pltpu.VMEM((quad_rows, keys), F32),
        ],
        compiler_params=PARAMS,
        cost_estimate=pl.CostEstimate(
            flops=4 * group * quad_rows * keys * HEAD_DIM,
            bytes_accessed=4 * quad_rows * width + 2 * keys * kv_width,
            transcendentals=group * quad_rows * keys,
        ),
        name="attend",
    )(*inputs)


def runs_kernel(ks, seq_count, ids, chosen, fresh, *rest):
    messages, outs = rest[: len(ks)], rest[len(ks) :]
    spans, block, _ = messages[0].shape
    run = outs[0].shape[2]
    me = ids[1] * KV_HEADS + ids[2]
    slab = len(outs) * run
    offset = ids[1] * slab

    def put(at, j, source, first):
        for m, out in enumerate(outs):
            if run % 16:
                rows = source[pl.ds(pl.multiple_of(first + offset, slab), slab), :].astype(F32)
                out[at, j] = rows[m * run : (m + 1) * run].astype(BF16)
            else:
                row = first + offset + (ids[0] ^ m) * run
                out[at, j] = source[pl.ds(pl.multiple_of(row, run), run), :]

    for at, k in enumerate(ks):
        for j in range(spans):
            put(at, j, messages[at].at[j], 0)
        for i in range(chosen.shape[1]):
            picked = chosen[0, i]

            @pl.when(picked % seq_count == me ^ k)
            def _():
                put(at, picked // seq_count, fresh, i * block)


def cut_runs(ks, seq_count, run, heads, ids, chosen, fresh, messages):
    spans, _, kv_width = messages[0].shape
    return pl.pallas_call(
        functools.partial(runs_kernel, ks, seq_count),
        out_shape=[jax.ShapeDtypeStruct((len(ks), spans, run, kv_width), BF16)] * heads,
        in_specs=[SMEM, SMEM, VMEM] + [VMEM] * len(ks),
        out_specs=[VMEM] * heads,
        compiler_params=PARAMS,
        name="runs",
    )(ids, chosen, fresh, *messages)


def lay_kernel(seq_count, pieces, ids, *rest):
    landed, out = rest[:-1], rest[-1]
    spans, run, width = landed[0].shape[1:]
    count = seq_count * spans * run
    blocks = spans * seq_count
    seat = ids[1] * KV_HEADS + ids[0]
    at = lax.broadcasted_iota(jnp.int32, (count, count), 1)
    source = seat ^ (at // (spans * run))
    target = (at % run) * blocks + (at // run) % spans * seq_count + source
    order = (lax.broadcasted_iota(jnp.int32, (count, count), 0) == target).astype(F32).astype(BF16)
    for k in range(len(landed) // pieces):
        parts = [landed[k * pieces + i][...] for i in range(pieces)]
        if run % 16:
            parts = [part.astype(F32) for part in parts]
        rows = jnp.concatenate([part.reshape(-1, width) for part in parts], axis=0).astype(BF16)
        laid = jnp.dot(order, rows, preferred_element_type=F32)
        request = ids[2] ^ k
        for u in range(run):
            out[0, 0, request, :, pl.ds(u * width, width)] = laid[u * blocks : (u + 1) * blocks].astype(BF16)


def join_kernel(ids, *rest):
    parts, out = rest[:-1], rest[-1]
    width = parts[0].shape[1]
    for d, part in enumerate(parts):
        out[0, :, pl.ds(pl.multiple_of((ids[2] ^ d) * width, HEAD_DIM), width)] = part[...]


def shards(pool_kv, span_home, span_order, chosen, fresh_q, fresh_kv):
    pool_count, quads, heads = (lax.axis_size(a) for a in ("pool", "quad", "head"))
    seq_count = quads * heads
    me, quad, head = (lax.axis_index(a) for a in ("pool", "quad", "head"))
    slots, block, width = pool_kv.shape
    spans = span_order.shape[1]
    rows, q_width = fresh_q.shape[1:]
    kv_width = width // heads
    q_part = q_width // heads
    run = block // seq_count
    ids = jnp.stack([me, quad, head]).astype(jnp.int32)
    seat = quad * heads + head

    packed = pl.pallas_call(
        functools.partial(pack_kernel, slots, spans),
        out_shape=[jax.ShapeDtypeStruct((block, width // 2), BF16)] * (2 * pool_count)
        + [jax.ShapeDtypeStruct((rows, q_part + kv_width), BF16)] * heads,
        in_specs=[SMEM, SMEM, HBM, HBM, HBM],
        out_specs=[ANY] * (2 * pool_count + heads),
        scratch_shapes=[pltpu.SemaphoreType.DMA((3, 2 * max(pool_count, heads)))],
        compiler_params=PARAMS,
        name="pack",
    )(ids, span_home, pool_kv, fresh_q, fresh_kv)
    to_pool = packed[:pool_count], packed[pool_count : 2 * pool_count]
    to_head = packed[2 * pool_count :]

    def swap(value, axes, count, k):
        return lax.ppermute(value, axes, [(i, i ^ k) for i in range(count)])

    def from_pool(values):
        arrived = [values[0]] + [None] * (pool_count - 1)
        for k in reversed(range(1, pool_count)):
            arrived[k] = swap(values[k], "pool", pool_count, k)
        return pl.pallas_call(
            functools.partial(choose_kernel, slots),
            out_shape=[jax.ShapeDtypeStruct((spans, block, kv_width), BF16)] * (heads // 2),
            in_specs=[SMEM, SMEM, SMEM] + [ANY] * pool_count,
            out_specs=[ANY] * (heads // 2),
            scratch_shapes=[pltpu.SemaphoreType.DMA((spans, heads // 2))],
            compiler_params=PARAMS,
            name="choose",
        )(ids, span_home, span_order, *arrived)

    seq = ("quad", "head")
    near_kv = from_pool(to_pool[0])
    gathered = [to_head[0]] + [swap(to_head[k], "head", heads, k) for k in range(1, heads)]
    q = jnp.concatenate(gathered, axis=0)
    far_kv = from_pool(to_pool[1])
    kv_out = [*near_kv, *far_kv]

    messages = [kv_out[0]] + [None] * (seq_count - 1)
    for k in range(1, seq_count):
        messages[k] = swap(kv_out[k % heads], seq, seq_count, k)

    own = q[:, q_part:]
    parts = [own] + [swap(own, "quad", quads, k) for k in range(1, quads)]
    listed = jnp.stack(parts).reshape(seq_count, rows, kv_width)
    fresh = jnp.take(listed, seat ^ jnp.arange(seq_count), axis=0).reshape(seq_count * rows, kv_width)

    groups = [[k, k + 1] for k in range(0, seq_count, 2)]
    state = None
    for ks in groups:
        state = attend(
            ks, state, ks is groups[-1], seq_count, rows, ids, chosen, q, fresh, [messages[k] for k in ks]
        )

    landed = []
    for ks in (range(seq_count - 2), range(seq_count - 2, seq_count)):
        cut = cut_runs(list(ks), seq_count, run, heads, ids, chosen, fresh, [messages[k] for k in ks])
        if run % 16:
            cut = [lax.dynamic_index_in_dim(jnp.stack(cut), me ^ k, axis=0, keepdims=False) for k in range(heads)]
        went = []
        for k in range(pool_count):
            perm = [
                ((r * quads + a) * heads + g, (g * quads + a) * heads + (r ^ k))
                for r in range(pool_count)
                for a in range(quads)
                for g in range(heads)
            ]
            went.append(lax.ppermute(cut[k], ("pool", "quad", "head"), perm))
        landed.append(went)
    decoded = pl.pallas_call(
        functools.partial(lay_kernel, seq_count, len(landed)),
        out_shape=jax.ShapeDtypeStruct((1, 1, pool_count, spans * seq_count, run * kv_width), BF16),
        in_specs=[SMEM] + [VMEM] * (len(landed) * pool_count),
        out_specs=VMEM,
        compiler_params=PARAMS,
        name="lay",
    )(ids, *[part for parts in zip(*landed) for part in parts])

    back = [state[0]] + [swap(state[k], "head", heads, k) for k in range(1, heads)]
    attended = pl.pallas_call(
        join_kernel,
        out_shape=jax.ShapeDtypeStruct((1, rows, q_width), BF16),
        in_specs=[SMEM] + [VMEM] * heads,
        out_specs=VMEM,
        compiler_params=PARAMS,
        name="join",
    )(ids, *back)
    return (attended, decoded)


def solution(mesh):
    pool_count, seq_count = mesh.shape["pool"], mesh.shape["seq"]
    fine = Mesh(mesh.devices.reshape(pool_count, seq_count // KV_HEADS, KV_HEADS), ("pool", "quad", "head"))
    seq = ("quad", "head")
    in_specs = (
        P("pool", seq, None),
        P(),
        P("pool", None),
        P("pool", None),
        P("pool", seq, None),
        P("pool", seq, None),
    )
    out_specs = (P("pool", seq, None), P("pool", seq, None, None, None))
    return jax.shard_map(shards, mesh=fine, in_specs=in_specs, out_specs=out_specs, check_vma=False)
```

```python
import functools
import math

import jax
import jax.numpy as jnp
from jax import lax
from jax.experimental import pallas as pl
from jax.experimental.pallas import tpu as pltpu
from jax.sharding import Mesh, PartitionSpec as P

KV_HEADS = 4
HEAD_DIM = 128
LOW = -1e30
HOME = 4
BF16 = jnp.bfloat16
F32 = jnp.float32

SMEM = pl.BlockSpec(memory_space=pltpu.SMEM)
VMEM = pl.BlockSpec(memory_space=pltpu.VMEM)
ANY = pl.BlockSpec(memory_space=pl.ANY)
HBM = pl.BlockSpec(memory_space=pltpu.HBM)
PARAMS = pltpu.CompilerParams(vmem_limit_bytes=40 * 1024 * 1024)
CHEAP = pl.CostEstimate(flops=1, bytes_accessed=1, transcendentals=1)
FULL = pltpu.CompilerParams(vmem_limit_bytes=60 * 1024 * 1024)


def turn(d):
    return (d & 1) * 3 ^ d >> 1


def pack_kernel(slots, spans, ids, pool_kv, *rest):
    outs, sems = rest[:-1], rest[-1]
    copies = []
    for d, out in enumerate(outs):
        slot = jnp.int32(0)
        for t in range(spans):
            held = ids[HOME + (ids[0] ^ d) * spans + t]
            slot = jnp.where(held // slots == ids[0], held % slots, slot)
        copies.append(pltpu.make_async_copy(pool_kv.at[slot], out, sems.at[d]))
        copies[-1].start()
    for copy in copies:
        copy.wait()


def split_kernel(ids, fresh_q, near, far, *rest):
    keep, give, send, sems = rest
    outs = (keep, give.at[0], send.at[0], send.at[1])
    q_width = fresh_q.shape[2] // KV_HEADS
    kv_width = near.shape[2] // KV_HEADS
    copies = []

    def copy(source, out, at):
        copies.append(pltpu.make_async_copy(source, out.at[:, at], sems.at[len(copies)]))
        copies[-1].start()

    for d, out in enumerate(outs):
        other = ids[3] ^ turn(d)
        q_at = pl.ds(pl.multiple_of(other * q_width, HEAD_DIM), q_width)
        kv_at = pl.ds(pl.multiple_of(other * kv_width, HEAD_DIM), kv_width)
        copy(fresh_q.at[0, :, q_at], out, pl.ds(0, q_width))
        copy(near.at[0, :, kv_at], out, pl.ds(q_width, kv_width))
        for a in range(far.shape[0]):
            copy(far.at[a, :, kv_at], out, pl.ds(q_width + (a + 1) * kv_width, kv_width))
    for each in copies:
        each.wait()


def arrays_of(views):
    arrays = []
    for array, _ in views:
        if not any(array is a for a in arrays):
            arrays.append(array)
    return arrays, [(next(i for i, a in enumerate(arrays) if a is array), index) for array, index in views]


def look(refs, views):
    return [refs[i] if index is None else refs[i].at[index] for i, index in views]


def sort_kernel(quads, views, ids, *rest):
    parts, out = look(rest[:-1], views), rest[-1]
    rows, width = parts[0].shape[0], out.shape[1]
    for d, part in enumerate(parts):
        for a in range(quads):
            seat = (ids[1] ^ a) * KV_HEADS + (ids[2] ^ d)
            first = part.shape[1] - (quads - a) * width
            out[pl.ds(pl.multiple_of(seat * rows, rows), rows), :] = part[:, first : first + width]


def choose_kernel(slots, pool_count, ids, *rest):
    arrived, (near, give, send), sems = rest[:pool_count], rest[pool_count:-1], rest[-1]
    outs = (near.at[0], give.at[0], send.at[0], give.at[1])
    spans, heads = sems.shape
    width = near.shape[3]
    for start in (True, False):
        for j in range(spans):
            source = (ids[HOME + ids[HOME + pool_count * spans + j]] // slots) ^ ids[0]
            for d in range(heads):
                at = pl.ds(pl.multiple_of((ids[3] ^ turn(d)) * width, HEAD_DIM), width)
                if start:
                    for p in range(pool_count):

                        @pl.when(source == p)
                        def _(p=p):
                            pltpu.make_async_copy(arrived[p].at[:, at], outs[d].at[j], sems.at[j, d]).start()

                else:
                    pltpu.make_async_copy(arrived[0].at[:, at], outs[d].at[j], sems.at[j, d]).wait()


def place_kernel(got, near_in, send_in, near, send):
    del near_in, send_in
    near[1] = got[0]
    send[1] = got[1]


def follow_kernel(got, give_in, give):
    del give_in
    give[1] = got[1]


def attend_kernel(ks, first, last, seq_count, rows, stacked, group, count_in, views, q_views, at_chosen, ids, fresh, *rest):
    messages, q = look(rest[:count_in], views), look(rest[:count_in], q_views)
    rest = rest[count_in:]
    spans, block, _ = messages[0].shape
    quad_rows = KV_HEADS * rows
    if not first:
        (acc_in, top_in, total_in), rest = rest[:3], rest[3:]
    outs, (keys, values, bias) = rest[:-3], rest[-3:]
    count = keys.shape[0]
    me = ids[1] * KV_HEADS + ids[2]

    values[:, HEAD_DIM:] = jnp.ones((count, HEAD_DIM), BF16)
    for at, k in enumerate(ks):
        for j in range(spans):
            row = pl.ds((at * spans + j) * block, block)
            keys[row, :] = messages[at][j, :, :HEAD_DIM]
            values[row, :HEAD_DIM] = messages[at][j, :, HEAD_DIM:]
        for i in range(ids.shape[0] - at_chosen):
            picked = ids[at_chosen + i]

            @pl.when(picked % seq_count == me ^ k)
            def _():
                row = pl.ds(pl.multiple_of((at * spans + picked // seq_count) * block, block), block)
                keys[row, :] = fresh[pl.ds(i * block, block), :HEAD_DIM]
                values[row, :HEAD_DIM] = fresh[pl.ds(i * block, block), HEAD_DIM:]

    local = lax.broadcasted_iota(jnp.int32, (quad_rows, 1), 0)
    listed = (ids[1] * KV_HEADS + (ids[2] ^ (local // rows))) * rows + local % rows
    which = listed // block
    place = jnp.zeros((quad_rows, 1), jnp.int32)
    for i in range(ids.shape[0] - at_chosen):
        place = jnp.where(which == i, ids[at_chosen + i] * block, place)
    place = place + listed % block
    for at, k in enumerate(ks):
        for j in range(spans):
            key = (j * seq_count + (me ^ k)) * block + lax.broadcasted_iota(jnp.int32, (quad_rows, block), 1)
            bias[:, pl.ds((at * spans + j) * block, block)] = jnp.where(key <= place, 0.0, LOW)

    scale = math.log2(math.e) / math.sqrt(HEAD_DIM)
    wide = stacked * quad_rows
    for h in range(0, group, stacked):
        cols = [pl.ds((h + i) * HEAD_DIM, HEAD_DIM) for i in range(stacked)]
        query = jnp.concatenate([part[:, c] for c in cols for part in q], axis=0)
        s = lax.dot_general(query, keys[...], (((1,), (1,)), ((), ())), preferred_element_type=F32)
        s = (s.reshape(stacked, quad_rows, count) * scale + bias[...][None]).reshape(wide, count)
        top = jnp.broadcast_to(jnp.max(s, axis=1, keepdims=True), (wide, HEAD_DIM))
        if not first:
            before = top_in[h // stacked]
            top = jnp.maximum(top, before)
        p = jnp.exp2(s - jnp.concatenate([top] * (count // HEAD_DIM), axis=1))
        both = jnp.dot(p.astype(BF16), values[...], preferred_element_type=F32)
        acc, total = both[:, :HEAD_DIM], both[:, HEAD_DIM:]
        if not first:
            factor = jnp.exp2(before - top)
            acc = acc + factor * acc_in[h // stacked]
            total = total + factor * total_in[h // stacked]
        if last:
            done = acc / total
            for i in range(stacked):
                for d in range(KV_HEADS):
                    at = i * quad_rows + d * rows
                    outs[d // 2][d % 2, :, cols[i]] = done[at : at + rows].astype(BF16)
        else:
            outs[0][h // stacked] = acc
            outs[1][h // stacked] = top
            outs[2][h // stacked] = total


def attend(ks, state, last, seq_count, rows, group, at_chosen, ids, q, fresh, messages):
    quad_rows = KV_HEADS * rows
    arrays, views = arrays_of([*messages, *q])
    spans, block, kv_width = messages[0][0].shape[-3:]
    keys = len(ks) * spans * block
    stacked = 2 - group % 2
    if last:
        out_shape = [jax.ShapeDtypeStruct((2, rows, group * HEAD_DIM), BF16)] * (KV_HEADS // 2)
    else:
        out_shape = [jax.ShapeDtypeStruct((group // stacked, stacked * quad_rows, HEAD_DIM), F32)] * 3
    inputs = [ids, fresh, *arrays, *(state or ())]
    return pl.pallas_call(
        functools.partial(
            attend_kernel,
            ks,
            state is None,
            last,
            seq_count,
            rows,
            stacked,
            group,
            len(arrays),
            views[: len(ks)],
            views[len(ks) :],
            at_chosen,
        ),
        out_shape=out_shape,
        in_specs=[SMEM] + [VMEM] * (len(inputs) - 1),
        out_specs=[VMEM] * len(out_shape),
        scratch_shapes=[
            pltpu.VMEM((keys, HEAD_DIM), BF16),
            pltpu.VMEM((keys, 2 * HEAD_DIM), BF16),
            pltpu.VMEM((quad_rows, keys), F32),
        ],
        compiler_params=PARAMS,
        cost_estimate=CHEAP,
        name="attend",
    )(*inputs)


def runs_kernel(ks, seq_count, count_in, views, at_chosen, ids, fresh, *rest):
    messages, outs = look(rest[:count_in], views), rest[count_in:]
    spans, block, _ = messages[0].shape
    run = outs[0].shape[2]
    me = ids[1] * KV_HEADS + ids[2]
    slab = len(outs) * run
    offset = ids[1] * slab

    def put(k, j, source, first):
        slot = ks.index(k) // KV_HEADS * KV_HEADS + (ids[2] ^ k % KV_HEADS)
        for m, out in enumerate(outs):
            if run % 16:
                rows = source[pl.ds(pl.multiple_of(first + offset, slab), slab), :].astype(F32)
                out[slot, j] = rows[m * run : (m + 1) * run].astype(BF16)
            else:
                row = first + offset + (ids[2] ^ m) * run
                out[slot, j] = source[pl.ds(pl.multiple_of(row, run), run), :]

    for at, k in enumerate(ks):
        for j in range(spans):
            put(k, j, messages[at].at[j], 0)
        for i in range(ids.shape[0] - at_chosen):
            picked = ids[at_chosen + i]

            @pl.when(picked % seq_count == me ^ k)
            def _():
                put(k, picked // seq_count, fresh, i * block)


def cut_runs(ks, seq_count, run, heads, at_chosen, ids, fresh, messages):
    arrays, views = arrays_of(messages)
    spans, _, kv_width = messages[0][0].shape[-3:]
    return pl.pallas_call(
        functools.partial(runs_kernel, ks, seq_count, len(arrays), views, at_chosen),
        out_shape=[jax.ShapeDtypeStruct((len(ks), spans, run, kv_width), BF16)] * heads,
        in_specs=[SMEM, VMEM] + [VMEM] * len(arrays),
        out_specs=[VMEM] * heads,
        compiler_params=PARAMS,
        cost_estimate=CHEAP,
        name="runs",
    )(ids, fresh, *arrays)


def lay_kernel(seq_count, parts, ids, *rest):
    landed, out = rest[:-1], rest[-1]
    spans, run, width = landed[0].shape[1:]
    count = seq_count * spans * run
    blocks = spans * seq_count
    at = lax.broadcasted_iota(jnp.int32, (count, count), 1)
    source = ids[1] * KV_HEADS ^ (at // (spans * run))
    target = (at % run) * blocks + (at // run) % spans * seq_count + source
    order = (lax.broadcasted_iota(jnp.int32, (count, count), 0) == target).astype(F32).astype(BF16)
    for k in range(KV_HEADS):
        rows = [landed[i * KV_HEADS + k][...] for i in range(parts)]
        if run % 16:
            rows = [part.astype(F32) for part in rows]
        rows = jnp.concatenate([part.reshape(-1, width) for part in rows], axis=0).astype(BF16)
        laid = jnp.dot(order, rows, preferred_element_type=F32)
        request = ids[0] ^ turn(ids[2] ^ k)
        for u in range(run):
            out[0, 0, request, :, pl.ds(u * width, width)] = laid[u * blocks : (u + 1) * blocks].astype(BF16)


def join_kernel(views, ids, *rest):
    parts, out = look(rest[:-1], views), rest[-1]
    width = parts[0].shape[1]
    for d, part in enumerate(parts):
        out[0, :, pl.ds(pl.multiple_of((ids[3] ^ turn(d)) * width, HEAD_DIM), width)] = part[...]


def shards(pool_kv, span_home, span_order, chosen, fresh_q, fresh_kv):
    pool_count, quads, heads = (lax.axis_size(a) for a in ("pool", "quad", "head"))
    seq_count = quads * heads
    me, quad, head = (lax.axis_index(a) for a in ("pool", "quad", "head"))
    slots, block, width = pool_kv.shape
    spans = span_order.shape[1]
    rows, q_width = fresh_q.shape[1:]
    kv_width = width // heads
    q_part = q_width // heads
    run = block // seq_count
    group = q_part // HEAD_DIM
    place = jnp.stack([me, quad, head, me ^ turn(head)]).astype(jnp.int32)
    ids = jnp.concatenate([place, span_home, span_order[0], chosen[0]])
    at_chosen = HOME + span_home.shape[0] + spans
    seat = quad * heads + head

    def after(value, *others):
        return lax.optimization_barrier((value, others))[0]

    def swap(value, axes, count, k):
        return lax.ppermute(value, axes, [(i, i ^ k) for i in range(count)])

    seq = ("quad", "head")
    to_pool = pl.pallas_call(
        functools.partial(pack_kernel, slots, spans),
        out_shape=[jax.ShapeDtypeStruct((block, width), BF16)] * pool_count,
        in_specs=[SMEM, ANY],
        out_specs=[ANY] * pool_count,
        scratch_shapes=[pltpu.SemaphoreType.DMA((pool_count,))],
        compiler_params=PARAMS,
        cost_estimate=CHEAP,
        name="pack",
    )(ids, pool_kv)
    far = [swap(after(fresh_kv, to_pool[0]), "quad", quads, k) for k in range(1, quads)]
    arrived = [to_pool[0]] + [None] * (pool_count - 1)
    for k in reversed(range(1, pool_count)):
        arrived[k] = swap(to_pool[k], "pool", pool_count, k)
    one = jax.ShapeDtypeStruct((rows, q_part + quads * kv_width), BF16)
    pair = jax.ShapeDtypeStruct((2, *one.shape), BF16)
    keep, give, send = pl.pallas_call(
        split_kernel,
        out_shape=[one, pair, pair],
        in_specs=[SMEM, ANY, ANY, ANY],
        out_specs=[ANY] * 3,
        scratch_shapes=[pltpu.SemaphoreType.DMA(((1 + quads) * heads,))],
        compiler_params=PARAMS,
        cost_estimate=CHEAP,
        name="split",
    )(ids, fresh_q, fresh_kv, far[0] if quads == 2 else jnp.concatenate(far, axis=0))
    chip = swap(send, "head", heads, 2)
    give = pl.pallas_call(
        follow_kernel,
        out_shape=pair,
        in_specs=[VMEM] * 2,
        out_specs=VMEM,
        input_output_aliases={1: 0},
        compiler_params=PARAMS,
        cost_estimate=CHEAP,
        name="follow",
    )(chip, give)
    core = swap(give, "head", heads, 1)
    q_give, q = give, [(keep, None), (core, 0), (chip, 0), (core, 1)]

    pair = jax.ShapeDtypeStruct((2, spans, block, kv_width), BF16)
    near, give, send = pl.pallas_call(
        functools.partial(choose_kernel, slots, pool_count),
        out_shape=[pair] * 3,
        in_specs=[SMEM] + [ANY] * pool_count,
        out_specs=[ANY] * 3,
        scratch_shapes=[pltpu.SemaphoreType.DMA((spans, heads))],
        compiler_params=PARAMS,
        cost_estimate=CHEAP,
        name="choose",
    )(ids, *after(arrived, send))

    def place(got, near, send):
        like = [jax.ShapeDtypeStruct(x.shape, x.dtype) for x in (near, send)]
        return pl.pallas_call(
            place_kernel,
            out_shape=like,
            in_specs=[VMEM] * 3,
            out_specs=[VMEM] * 2,
            input_output_aliases={1: 0, 2: 1},
            compiler_params=PARAMS,
            cost_estimate=CHEAP,
            name="place",
        )(got, near, send)

    near, send = place(after(swap(give, "head", heads, 1), q_give), near, send)
    rest = swap(send, "head", heads, 2)
    messages = [(near, 0), (near, 1), (rest, 0), (rest, 1)]

    if rows % 16:
        q = [(jnp.concatenate([part if index is None else part[index] for part, index in q], axis=0), None)]
        listed = q[0][0][:, q_part:].reshape(heads, rows, quads, kv_width).transpose(2, 0, 1, 3)
        listed = listed.reshape(seq_count, rows, kv_width)
        fresh = jnp.take(listed, seat ^ jnp.arange(seq_count), axis=0).reshape(seq_count * rows, kv_width)
    else:
        arrays, views = arrays_of(q)
        fresh = pl.pallas_call(
            functools.partial(sort_kernel, quads, views),
            out_shape=jax.ShapeDtypeStruct((seq_count * rows, kv_width), BF16),
            in_specs=[SMEM] + [VMEM] * len(arrays),
            out_specs=VMEM,
            compiler_params=PARAMS,
            cost_estimate=CHEAP,
            name="sort",
        )(ids, *arrays)

    def to_decode(ks, *dep):
        arrays, views = arrays_of([messages[k] for k in ks])
        arrays = after(arrays, dep)
        parts = [(arrays[i], index) for i, index in views]
        cut = cut_runs(ks, seq_count, run, heads, at_chosen, ids, fresh, parts)
        if run % 16:
            cut = [lax.dynamic_index_in_dim(jnp.stack(cut), head ^ k, axis=0, keepdims=False) for k in range(heads)]
        went = [None] * heads
        for k in reversed(range(heads)):
            perm = [
                ((r * quads + a) * heads + i, ((r ^ turn(i)) * quads + a) * heads + (i ^ k))
                for r in range(pool_count)
                for a in range(quads)
                for i in range(heads)
            ]
            went[k] = lax.ppermute(cut[k], ("pool", "quad", "head"), perm)
        return went, cut

    def work(ks, state, last=False):
        return attend(ks, state, last, seq_count, rows, group, at_chosen, ids, q, fresh, [messages[k] for k in ks])

    for a in range(1, quads):
        for half in (near, rest):
            crossed = swap(half, "quad", quads, a)
            messages += [(crossed, 0), (crossed, 1)]
    state = work(list(range(heads)), None)
    groups = [[k, k + 1] for k in range(heads, seq_count, 2)]
    far_ks = list(range(seq_count - heads, seq_count))
    for ks in groups[:-1]:
        if ks[0] == far_ks[0]:
            landed = [to_decode(list(range(far_ks[0])), state)]
            state = after(state, landed[0][1])
        state = work(ks, state)
    kept, sent = work(groups[-1], state, True)
    chip = swap(after(sent, landed[0][0]), "head", heads, 2)
    landed.append(to_decode(far_ks, kept))
    chip = after(chip, landed[1][0])
    core = swap(jnp.stack([kept[1], chip[1]]), "head", heads, 1)
    arrays, views = arrays_of([(kept, 0), (core, 0), (chip, 0), (core, 1)])
    attended = pl.pallas_call(
        functools.partial(join_kernel, views),
        out_shape=jax.ShapeDtypeStruct((1, rows, q_width), BF16),
        in_specs=[SMEM] + [VMEM] * len(arrays),
        out_specs=VMEM,
        compiler_params=PARAMS,
        cost_estimate=CHEAP,
        name="join",
    )(ids, *arrays)
    arrays = [part for went, _ in landed for part in went]
    decoded = pl.pallas_call(
        functools.partial(lay_kernel, seq_count, len(landed)),
        out_shape=jax.ShapeDtypeStruct((1, 1, pool_count, spans * seq_count, run * kv_width), BF16),
        in_specs=[SMEM] + [VMEM] * len(arrays),
        out_specs=VMEM,
        compiler_params=PARAMS,
        cost_estimate=CHEAP,
        name="lay",
    )(ids, *arrays)
    return (attended, decoded)


def solution(mesh):
    pool_count, seq_count = mesh.shape["pool"], mesh.shape["seq"]
    fine = Mesh(mesh.devices.reshape(pool_count, seq_count // KV_HEADS, KV_HEADS), ("pool", "quad", "head"))
    seq = ("quad", "head")
    in_specs = (
        P("pool", seq, None),
        P(),
        P("pool", None),
        P("pool", None),
        P("pool", seq, None),
        P("pool", seq, None),
    )
    out_specs = (P("pool", seq, None), P("pool", seq, None, None, None))
    return jax.shard_map(shards, mesh=fine, in_specs=in_specs, out_specs=out_specs, check_vma=False)
```

```python
import functools
import math

import jax
import jax.numpy as jnp
from jax import lax
from jax.experimental import pallas as pl
from jax.experimental.pallas import tpu as pltpu
from jax.sharding import Mesh, PartitionSpec as P

KV_HEADS = 4
HEAD_DIM = 128
LOW = -1e30
HOME = 4
BF16 = jnp.bfloat16
F32 = jnp.float32

SMEM = pl.BlockSpec(memory_space=pltpu.SMEM)
VMEM = pl.BlockSpec(memory_space=pltpu.VMEM)
ANY = pl.BlockSpec(memory_space=pl.ANY)
HBM = pl.BlockSpec(memory_space=pltpu.HBM)
PARAMS = pltpu.CompilerParams(vmem_limit_bytes=40 * 1024 * 1024)
CHEAP = pl.CostEstimate(flops=1, bytes_accessed=1, transcendentals=1)
FULL = pltpu.CompilerParams(vmem_limit_bytes=60 * 1024 * 1024)


def turn(d):
    return (d & 1) * 3 ^ d >> 1


def pack_kernel(slots, spans, ids, pool_kv, *rest):
    pool_count = (len(rest) - 1) // 2
    first, others, sems = rest[:pool_count], rest[pool_count:-1], rest[-1]
    width = first[0].shape[1]
    copies = []
    for d in range(pool_count):
        slot = jnp.int32(0)
        for t in range(spans):
            held = ids[HOME + (ids[0] ^ d) * spans + t]
            slot = jnp.where(held // slots == ids[0], held % slots, slot)
        for n in range(KV_HEADS):
            source = pool_kv.at[slot, :, pl.ds(pl.multiple_of((ids[3] ^ d ^ turn(n)) * width, HEAD_DIM), width)]
            out = others[d].at[:, pl.ds((n - 1) * width, width)] if n else first[d]
            copies.append(pltpu.make_async_copy(source, out, sems.at[d, n]))
            copies[-1].start()
    for copy in copies:
        copy.wait()


def split_kernel(ids, fresh_q, near, far, *rest):
    keep, give, send, sems = rest
    outs = (keep, give.at[0], send.at[0], send.at[1])
    q_width = fresh_q.shape[2] // KV_HEADS
    kv_width = near.shape[2] // KV_HEADS
    copies = []

    def copy(source, out, at):
        copies.append(pltpu.make_async_copy(source, out.at[:, at], sems.at[len(copies)]))
        copies[-1].start()

    for d, out in enumerate(outs):
        other = ids[3] ^ turn(d)
        q_at = pl.ds(pl.multiple_of(other * q_width, HEAD_DIM), q_width)
        kv_at = pl.ds(pl.multiple_of(other * kv_width, HEAD_DIM), kv_width)
        copy(fresh_q.at[0, :, q_at], out, pl.ds(0, q_width))
        copy(near.at[0, :, kv_at], out, pl.ds(q_width, kv_width))
        for a in range(far.shape[0]):
            copy(far.at[a, :, kv_at], out, pl.ds(q_width + (a + 1) * kv_width, kv_width))
    for each in copies:
        each.wait()


def arrays_of(views):
    arrays = []
    for array, _ in views:
        if not any(array is a for a in arrays):
            arrays.append(array)
    return arrays, [(next(i for i, a in enumerate(arrays) if a is array), index) for array, index in views]


def look(refs, views):
    return [refs[i] if index is None else refs[i].at[index] for i, index in views]


def sort_kernel(quads, views, ids, *rest):
    parts, out = look(rest[:-1], views), rest[-1]
    rows, width = parts[0].shape[0], out.shape[1]
    for d, part in enumerate(parts):
        for a in range(quads):
            seat = (ids[1] ^ a) * KV_HEADS + (ids[2] ^ d)
            first = part.shape[1] - (quads - a) * width
            out[pl.ds(pl.multiple_of(seat * rows, rows), rows), :] = part[:, first : first + width]


def choose_kernel(slots, pool_count, ids, *rest):
    arrived, outs, sems = rest[:pool_count], rest[pool_count:-1], rest[-1]
    if len(outs) == 2:
        give, send = outs
        outs = (give.at[0], send.at[0], give.at[1])
    spans = sems.shape[0]
    width = outs[0].shape[2]
    for start in (True, False):
        for j in range(spans):
            source = (ids[HOME + ids[HOME + pool_count * spans + j]] // slots) ^ ids[0]
            for n, out in enumerate(outs):
                at = pl.ds(n * width, width)
                if start:
                    for p in range(pool_count):

                        @pl.when(source == p)
                        def _(p=p):
                            pltpu.make_async_copy(arrived[p].at[:, at], out.at[j], sems.at[j, n]).start()

                else:
                    pltpu.make_async_copy(arrived[0].at[:, at], out.at[j], sems.at[j, n]).wait()


def place_kernel(got, send_in, beside, send):
    del send_in
    beside[...] = got[0]
    send[1] = got[1]


def follow_kernel(got, give_in, give):
    del give_in
    give[1] = got[1]


def attend_kernel(ks, first, last, seq_count, rows, stacked, group, count_in, views, q_views, at_chosen, ids, fresh, *rest):
    messages, q = look(rest[:count_in], views), look(rest[:count_in], q_views)
    rest = rest[count_in:]
    spans, block, _ = messages[0].shape
    quad_rows = KV_HEADS * rows
    if not first:
        (acc_in, top_in, total_in), rest = rest[:3], rest[3:]
    outs, (keys, values, bias) = rest[:-3], rest[-3:]
    count = keys.shape[0]
    me = ids[1] * KV_HEADS + ids[2]

    values[:, HEAD_DIM:] = jnp.ones((count, HEAD_DIM), BF16)
    for at, k in enumerate(ks):
        for j in range(spans):
            row = pl.ds((at * spans + j) * block, block)
            keys[row, :] = messages[at][j, :, :HEAD_DIM]
            values[row, :HEAD_DIM] = messages[at][j, :, HEAD_DIM:]
        for i in range(ids.shape[0] - at_chosen):
            picked = ids[at_chosen + i]

            @pl.when(picked % seq_count == me ^ k)
            def _():
                row = pl.ds(pl.multiple_of((at * spans + picked // seq_count) * block, block), block)
                keys[row, :] = fresh[pl.ds(i * block, block), :HEAD_DIM]
                values[row, :HEAD_DIM] = fresh[pl.ds(i * block, block), HEAD_DIM:]

    local = lax.broadcasted_iota(jnp.int32, (quad_rows, 1), 0)
    listed = (ids[1] * KV_HEADS + (ids[2] ^ (local // rows))) * rows + local % rows
    which = listed // block
    place = jnp.zeros((quad_rows, 1), jnp.int32)
    for i in range(ids.shape[0] - at_chosen):
        place = jnp.where(which == i, ids[at_chosen + i] * block, place)
    place = place + listed % block
    for at, k in enumerate(ks):
        for j in range(spans):
            key = (j * seq_count + (me ^ k)) * block + lax.broadcasted_iota(jnp.int32, (quad_rows, block), 1)
            bias[:, pl.ds((at * spans + j) * block, block)] = jnp.where(key <= place, 0.0, LOW)

    scale = math.log2(math.e) / math.sqrt(HEAD_DIM)
    wide = stacked * quad_rows
    for h in range(0, group, stacked):
        cols = [pl.ds((h + i) * HEAD_DIM, HEAD_DIM) for i in range(stacked)]
        query = jnp.concatenate([part[:, c] for c in cols for part in q], axis=0)
        s = lax.dot_general(query, keys[...], (((1,), (1,)), ((), ())), preferred_element_type=F32)
        s = (s.reshape(stacked, quad_rows, count) * scale + bias[...][None]).reshape(wide, count)
        top = jnp.broadcast_to(jnp.max(s, axis=1, keepdims=True), (wide, HEAD_DIM))
        if not first:
            before = top_in[h // stacked]
            top = jnp.maximum(top, before)
        p = jnp.exp2(s - jnp.concatenate([top] * (count // HEAD_DIM), axis=1))
        both = jnp.dot(p.astype(BF16), values[...], preferred_element_type=F32)
        acc, total = both[:, :HEAD_DIM], both[:, HEAD_DIM:]
        if not first:
            factor = jnp.exp2(before - top)
            acc = acc + factor * acc_in[h // stacked]
            total = total + factor * total_in[h // stacked]
        if last:
            done = acc / total
            for i in range(stacked):
                for d in range(KV_HEADS):
                    at = i * quad_rows + d * rows
                    outs[d // 2][d % 2, :, cols[i]] = done[at : at + rows].astype(BF16)
        else:
            outs[0][h // stacked] = acc
            outs[1][h // stacked] = top
            outs[2][h // stacked] = total


def attend(ks, state, last, seq_count, rows, group, at_chosen, ids, q, fresh, messages):
    quad_rows = KV_HEADS * rows
    arrays, views = arrays_of([*messages, *q])
    spans, block, kv_width = messages[0][0].shape[-3:]
    keys = len(ks) * spans * block
    stacked = 2 - group % 2
    if last:
        out_shape = [jax.ShapeDtypeStruct((2, rows, group * HEAD_DIM), BF16)] * (KV_HEADS // 2)
    else:
        out_shape = [jax.ShapeDtypeStruct((group // stacked, stacked * quad_rows, HEAD_DIM), F32)] * 3
    inputs = [ids, fresh, *arrays, *(state or ())]
    return pl.pallas_call(
        functools.partial(
            attend_kernel,
            ks,
            state is None,
            last,
            seq_count,
            rows,
            stacked,
            group,
            len(arrays),
            views[: len(ks)],
            views[len(ks) :],
            at_chosen,
        ),
        out_shape=out_shape,
        in_specs=[SMEM] + [VMEM] * (len(inputs) - 1),
        out_specs=[VMEM] * len(out_shape),
        scratch_shapes=[
            pltpu.VMEM((keys, HEAD_DIM), BF16),
            pltpu.VMEM((keys, 2 * HEAD_DIM), BF16),
            pltpu.VMEM((quad_rows, keys), F32),
        ],
        compiler_params=PARAMS,
        cost_estimate=CHEAP,
        name="attend",
    )(*inputs)


def slot_of(ks, k, head):
    at = ks.index(k)
    whole = min(KV_HEADS, len(ks) - at // KV_HEADS * KV_HEADS)
    return at // KV_HEADS * KV_HEADS + ((head ^ k) & (whole - 1))


def runs_kernel(ks, seq_count, count_in, views, at_chosen, ids, fresh, *rest):
    messages, outs = look(rest[:count_in], views), rest[count_in:]
    spans, block, _ = messages[0].shape
    run = outs[0].shape[2]
    me = ids[1] * KV_HEADS + ids[2]
    slab = len(outs) * run
    offset = ids[1] * slab

    def put(k, j, source, first):
        slot = slot_of(ks, k, ids[2])
        for m, out in enumerate(outs):
            if run % 16:
                rows = source[pl.ds(pl.multiple_of(first + offset, slab), slab), :].astype(F32)
                out[slot, j] = rows[m * run : (m + 1) * run].astype(BF16)
            else:
                row = first + offset + (ids[2] ^ m) * run
                out[slot, j] = source[pl.ds(pl.multiple_of(row, run), run), :]

    for at, k in enumerate(ks):
        for j in range(spans):
            put(k, j, messages[at].at[j], 0)
        for i in range(ids.shape[0] - at_chosen):
            picked = ids[at_chosen + i]

            @pl.when(picked % seq_count == me ^ k)
            def _():
                put(k, picked // seq_count, fresh, i * block)


def cut_runs(ks, seq_count, run, heads, at_chosen, ids, fresh, messages):
    arrays, views = arrays_of(messages)
    spans, _, kv_width = messages[0][0].shape[-3:]
    return pl.pallas_call(
        functools.partial(runs_kernel, ks, seq_count, len(arrays), views, at_chosen),
        out_shape=[jax.ShapeDtypeStruct((len(ks), spans, run, kv_width), BF16)] * heads,
        in_specs=[SMEM, VMEM] + [VMEM] * len(arrays),
        out_specs=[VMEM] * heads,
        compiler_params=PARAMS,
        cost_estimate=CHEAP,
        name="runs",
    )(ids, fresh, *arrays)


def lay_kernel(seq_count, parts, ids, *rest):
    landed, out = rest[:-1], rest[-1]
    spans, run, width = landed[0].shape[1:]
    count = seq_count * spans * run
    blocks = spans * seq_count
    at = lax.broadcasted_iota(jnp.int32, (count, count), 1)
    to = lax.broadcasted_iota(jnp.int32, (count, count), 0)

    def order_of(sender):
        source = at // (spans * run)
        half = jnp.where(source < seq_count - KV_HEADS, 0, sender & KV_HEADS // 2)
        target = (at % run) * blocks + (at // run) % spans * seq_count + (ids[1] * KV_HEADS ^ source ^ half)
        return (to == target).astype(F32).astype(BF16)

    for k in range(KV_HEADS):
        if k % (KV_HEADS // 2) == 0:
            order = order_of(ids[2] ^ k)
        rows = [landed[i * KV_HEADS + k][...] for i in range(parts)]
        if run % 16:
            rows = [part.astype(F32) for part in rows]
        rows = jnp.concatenate([part.reshape(-1, width) for part in rows], axis=0).astype(BF16)
        laid = jnp.dot(order, rows, preferred_element_type=F32)
        request = ids[0] ^ turn(ids[2] ^ k)
        for u in range(run):
            out[0, 0, request, :, pl.ds(u * width, width)] = laid[u * blocks : (u + 1) * blocks].astype(BF16)


def join_kernel(views, ids, *rest):
    parts, out = look(rest[:-1], views), rest[-1]
    width = parts[0].shape[1]
    for d, part in enumerate(parts):
        out[0, :, pl.ds(pl.multiple_of((ids[3] ^ turn(d)) * width, HEAD_DIM), width)] = part[...]


def shards(pool_kv, span_home, span_order, chosen, fresh_q, fresh_kv):
    pool_count, quads, heads = (lax.axis_size(a) for a in ("pool", "quad", "head"))
    seq_count = quads * heads
    me, quad, head = (lax.axis_index(a) for a in ("pool", "quad", "head"))
    slots, block, width = pool_kv.shape
    spans = span_order.shape[1]
    rows, q_width = fresh_q.shape[1:]
    kv_width = width // heads
    q_part = q_width // heads
    run = block // seq_count
    group = q_part // HEAD_DIM
    place = jnp.stack([me, quad, head, me ^ turn(head)]).astype(jnp.int32)
    ids = jnp.concatenate([place, span_home, span_order[0], chosen[0]])
    at_chosen = HOME + span_home.shape[0] + spans
    seat = quad * heads + head

    def after(value, *others):
        return lax.optimization_barrier((value, others))[0]

    def swap(value, axes, count, k):
        return lax.ppermute(value, axes, [(i, i ^ k) for i in range(count)])

    seq = ("quad", "head")
    to_pool = pl.pallas_call(
        functools.partial(pack_kernel, slots, spans),
        out_shape=[jax.ShapeDtypeStruct((block, kv_width), BF16)] * pool_count
        + [jax.ShapeDtypeStruct((block, width - kv_width), BF16)] * pool_count,
        in_specs=[SMEM, ANY],
        out_specs=[ANY] * (2 * pool_count),
        scratch_shapes=[pltpu.SemaphoreType.DMA((pool_count, heads))],
        compiler_params=PARAMS,
        cost_estimate=CHEAP,
        name="pack",
    )(ids, pool_kv)
    far = [swap(after(fresh_kv, to_pool[0]), "quad", quads, k) for k in range(1, quads)]

    def from_pool(values, out_shape, *dep):
        arrived = [values[0]] + [None] * (pool_count - 1)
        for k in reversed(range(1, pool_count)):
            arrived[k] = swap(values[k], "pool", pool_count, k)
        return pl.pallas_call(
            functools.partial(choose_kernel, slots, pool_count),
            out_shape=out_shape,
            in_specs=[SMEM] + [ANY] * pool_count,
            out_specs=[ANY] * len(out_shape),
            scratch_shapes=[pltpu.SemaphoreType.DMA((spans, heads - 1))],
            compiler_params=PARAMS,
            cost_estimate=CHEAP,
            name="choose",
        )(ids, *after(arrived, dep))

    blocks = jax.ShapeDtypeStruct((spans, block, kv_width), BF16)
    (own,) = from_pool(to_pool[:pool_count], [blocks], far)
    early = [swap(own, "quad", quads, a) for a in range(1, quads)]
    one = jax.ShapeDtypeStruct((rows, q_part + quads * kv_width), BF16)
    pair = jax.ShapeDtypeStruct((2, *one.shape), BF16)
    keep, give, send = pl.pallas_call(
        split_kernel,
        out_shape=[one, pair, pair],
        in_specs=[SMEM, ANY, ANY, ANY],
        out_specs=[ANY] * 3,
        scratch_shapes=[pltpu.SemaphoreType.DMA(((1 + quads) * heads,))],
        compiler_params=PARAMS,
        cost_estimate=CHEAP,
        name="split",
    )(ids, fresh_q, fresh_kv, far[0] if quads == 2 else jnp.concatenate(far, axis=0))
    chip = swap(send, "head", heads, 2)
    give = pl.pallas_call(
        follow_kernel,
        out_shape=pair,
        in_specs=[VMEM] * 2,
        out_specs=VMEM,
        input_output_aliases={1: 0},
        compiler_params=PARAMS,
        cost_estimate=CHEAP,
        name="follow",
    )(chip, give)
    core = swap(give, "head", heads, 1)
    q_give, q = give, [(keep, None), (core, 0), (chip, 0), (core, 1)]

    pair = jax.ShapeDtypeStruct((2, *blocks.shape), BF16)
    give, kv_send = from_pool(to_pool[pool_count:], [pair] * 2, send, early)
    beside, kv_send = pl.pallas_call(
        place_kernel,
        out_shape=[blocks, pair],
        in_specs=[VMEM] * 2,
        out_specs=[VMEM] * 2,
        input_output_aliases={1: 1},
        compiler_params=PARAMS,
        cost_estimate=CHEAP,
        name="place",
    )(after(swap(give, "head", heads, 1), q_give), kv_send)
    rest = swap(kv_send, "head", heads, 2)
    messages = [(own, None), (beside, None), (rest, 0), (rest, 1)]

    if rows % 16:
        q = [(jnp.concatenate([part if index is None else part[index] for part, index in q], axis=0), None)]
        listed = q[0][0][:, q_part:].reshape(heads, rows, quads, kv_width).transpose(2, 0, 1, 3)
        listed = listed.reshape(seq_count, rows, kv_width)
        fresh = jnp.take(listed, seat ^ jnp.arange(seq_count), axis=0).reshape(seq_count * rows, kv_width)
    else:
        arrays, views = arrays_of(q)
        fresh = pl.pallas_call(
            functools.partial(sort_kernel, quads, views),
            out_shape=jax.ShapeDtypeStruct((seq_count * rows, kv_width), BF16),
            in_specs=[SMEM] + [VMEM] * len(arrays),
            out_specs=VMEM,
            compiler_params=PARAMS,
            cost_estimate=CHEAP,
            name="sort",
        )(ids, *arrays)

    def to_decode(ks, *dep):
        arrays, views = arrays_of([messages[k] for k in ks])
        arrays = after(arrays, dep)
        parts = [(arrays[i], index) for i, index in views]
        cut = cut_runs(ks, seq_count, run, heads, at_chosen, ids, fresh, parts)
        if run % 16:
            cut = [lax.dynamic_index_in_dim(jnp.stack(cut), head ^ k, axis=0, keepdims=False) for k in range(heads)]
        went = [None] * heads
        for k in reversed(range(heads)):
            perm = [
                ((r * quads + a) * heads + i, ((r ^ turn(i)) * quads + a) * heads + (i ^ k))
                for r in range(pool_count)
                for a in range(quads)
                for i in range(heads)
            ]
            went[k] = lax.ppermute(cut[k], ("pool", "quad", "head"), perm)
        return went, cut

    def work(ks, state, last=False):
        return attend(ks, state, last, seq_count, rows, group, at_chosen, ids, q, fresh, [messages[k] for k in ks])

    for a in range(1, quads):
        second = swap(beside, "quad", quads, a)
        crossed = swap(after(rest, second), "quad", quads, a)
        messages += [(early[a - 1], None), (second, None), (crossed, 0), (crossed, 1)]
    groups = [list(range(seq_count - 2)), [seq_count - 2, seq_count - 1]]
    landed = [to_decode(groups[0])]
    fresh = after(fresh, landed[0][1])
    state = None
    for first in range(0, seq_count - 2, 6):
        state = work(groups[0][first : first + 6], state)
    kept, sent = work(groups[-1], state, True)
    chip = swap(after(sent, landed[0][0]), "head", heads, 2)
    landed.append(to_decode(groups[1], kept))
    chip = after(chip, landed[1][0])
    core = swap(jnp.stack([kept[1], chip[1]]), "head", heads, 1)
    arrays, views = arrays_of([(kept, 0), (core, 0), (chip, 0), (core, 1)])
    attended = pl.pallas_call(
        functools.partial(join_kernel, views),
        out_shape=jax.ShapeDtypeStruct((1, rows, q_width), BF16),
        in_specs=[SMEM] + [VMEM] * len(arrays),
        out_specs=VMEM,
        compiler_params=PARAMS,
        cost_estimate=CHEAP,
        name="join",
    )(ids, *arrays)
    arrays = [part for went, _ in landed for part in went]
    decoded = pl.pallas_call(
        functools.partial(lay_kernel, seq_count, len(landed)),
        out_shape=jax.ShapeDtypeStruct((1, 1, pool_count, spans * seq_count, run * kv_width), BF16),
        in_specs=[SMEM] + [VMEM] * len(arrays),
        out_specs=VMEM,
        compiler_params=PARAMS,
        cost_estimate=CHEAP,
        name="lay",
    )(ids, *arrays)
    return (attended, decoded)


def solution(mesh):
    pool_count, seq_count = mesh.shape["pool"], mesh.shape["seq"]
    fine = Mesh(mesh.devices.reshape(pool_count, seq_count // KV_HEADS, KV_HEADS), ("pool", "quad", "head"))
    seq = ("quad", "head")
    in_specs = (
        P("pool", seq, None),
        P(),
        P("pool", None),
        P("pool", None),
        P("pool", seq, None),
        P("pool", seq, None),
    )
    out_specs = (P("pool", seq, None), P("pool", seq, None, None, None))
    return jax.shard_map(shards, mesh=fine, in_specs=in_specs, out_specs=out_specs, check_vma=False)
```

```python
import functools
import math

import jax
import jax.numpy as jnp
from jax import lax
from jax.experimental import pallas as pl
from jax.experimental.pallas import tpu as pltpu
from jax.sharding import Mesh, PartitionSpec as P

KV_HEADS = 4
HEAD_DIM = 128
LOW = -1e30
HOME = 4
BF16 = jnp.bfloat16
F32 = jnp.float32

SMEM = pl.BlockSpec(memory_space=pltpu.SMEM)
VMEM = pl.BlockSpec(memory_space=pltpu.VMEM)
ANY = pl.BlockSpec(memory_space=pl.ANY)
HBM = pl.BlockSpec(memory_space=pltpu.HBM)
PARAMS = pltpu.CompilerParams(vmem_limit_bytes=40 * 1024 * 1024)
CHEAP = pl.CostEstimate(flops=1, bytes_accessed=1, transcendentals=1)
FULL = pltpu.CompilerParams(vmem_limit_bytes=60 * 1024 * 1024)


def turn(d):
    return (d & 1) * 3 ^ d >> 1


def pack_kernel(slots, spans, ids, pool_kv, *rest):
    pool_count = (len(rest) - 1) // 2
    first, others, sems = rest[:pool_count], rest[pool_count:-1], rest[-1]
    width = first[0].shape[1]
    copies = []
    for d in range(pool_count):
        slot = jnp.int32(0)
        for t in range(spans):
            held = ids[HOME + (ids[0] ^ d) * spans + t]
            slot = jnp.where(held // slots == ids[0], held % slots, slot)
        for n in range(KV_HEADS):
            source = pool_kv.at[slot, :, pl.ds(pl.multiple_of((ids[3] ^ d ^ turn(n)) * width, HEAD_DIM), width)]
            out = others[d].at[:, pl.ds((n - 1) * width, width)] if n else first[d]
            copies.append(pltpu.make_async_copy(source, out, sems.at[d, n]))
            copies[-1].start()
    for copy in copies:
        copy.wait()


def split_kernel(ids, fresh_q, near, far, *rest):
    keep, give, send, sems = rest
    outs = (keep, give.at[0], send.at[0], send.at[1])
    q_width = fresh_q.shape[2] // KV_HEADS
    kv_width = near.shape[2] // KV_HEADS
    copies = []

    def copy(source, out, at):
        copies.append(pltpu.make_async_copy(source, out.at[:, at], sems.at[len(copies)]))
        copies[-1].start()

    for d, out in enumerate(outs):
        other = ids[3] ^ turn(d)
        q_at = pl.ds(pl.multiple_of(other * q_width, HEAD_DIM), q_width)
        kv_at = pl.ds(pl.multiple_of(other * kv_width, HEAD_DIM), kv_width)
        copy(fresh_q.at[0, :, q_at], out, pl.ds(0, q_width))
        copy(near.at[0, :, kv_at], out, pl.ds(q_width, kv_width))
        for a in range(far.shape[0]):
            copy(far.at[a, :, kv_at], out, pl.ds(q_width + (a + 1) * kv_width, kv_width))
    for each in copies:
        each.wait()


def arrays_of(views):
    arrays = []
    for array, _ in views:
        if not any(array is a for a in arrays):
            arrays.append(array)
    return arrays, [(next(i for i, a in enumerate(arrays) if a is array), index) for array, index in views]


def look(refs, views):
    return [refs[i] if index is None else refs[i].at[index] for i, index in views]


def ahead(seat):
    return (seat // (KV_HEADS // 2) ^ seat // KV_HEADS) & 1


def arrived_of(refs, seat):
    if len(refs) == 1:
        return lambda at: refs[0][at]
    return lambda at: jnp.where(ahead(seat) == 1, refs[0][at], refs[1][at])


def group_views(views, messages):
    views = iter(views)
    return [[next(views) for _ in message] for message in messages]


def sort_kernel(quads, views, ids, *rest):
    parts, out = look(rest[:-1], views), rest[-1]
    rows, width = parts[0].shape[0], out.shape[1]
    for d, part in enumerate(parts):
        for a in range(quads):
            seat = (ids[1] ^ a) * KV_HEADS + (ids[2] ^ d)
            first = part.shape[1] - (quads - a) * width
            out[pl.ds(pl.multiple_of(seat * rows, rows), rows), :] = part[:, first : first + width]


def choose_kernel(slots, pool_count, ids, *rest):
    arrived, outs, sems = rest[:pool_count], rest[pool_count:-1], rest[-1]
    if len(outs) == 2:
        give, send = outs
        outs = (give.at[0], send.at[0], give.at[1])
    spans = sems.shape[0]
    width = outs[0].shape[2]
    for start in (True, False):
        for j in range(spans):
            source = (ids[HOME + ids[HOME + pool_count * spans + j]] // slots) ^ ids[0]
            for n, out in enumerate(outs):
                at = pl.ds(n * width, width)
                if start:
                    for p in range(pool_count):

                        @pl.when(source == p)
                        def _(p=p):
                            pltpu.make_async_copy(arrived[p].at[:, at], out.at[j], sems.at[j, n]).start()

                else:
                    pltpu.make_async_copy(arrived[0].at[:, at], out.at[j], sems.at[j, n]).wait()


def place_kernel(got, send_in, beside, send):
    del send_in
    beside[...] = got[0]
    send[1] = got[1]


def follow_kernel(got, give_in, give):
    del give_in
    give[1] = got[1]


def attend_kernel(ks, first, last, seq_count, rows, stacked, group, count_in, views, q_views, at_chosen, ids, fresh, *rest):
    messages, q = [look(rest[:count_in], v) for v in views], look(rest[:count_in], q_views)
    rest = rest[count_in:]
    spans, block, _ = messages[0][0].shape
    quad_rows = KV_HEADS * rows
    if not first:
        (acc_in, top_in, total_in), rest = rest[:3], rest[3:]
    outs, (keys, values, bias) = rest[:-3], rest[-3:]
    count = keys.shape[0]
    me = ids[1] * KV_HEADS + ids[2]

    values[:, HEAD_DIM:] = jnp.ones((count, HEAD_DIM), BF16)
    for at, k in enumerate(ks):
        for j in range(spans):
            row = pl.ds((at * spans + j) * block, block)
            both = arrived_of(messages[at], me ^ k)(j)
            keys[row, :] = both[:, :HEAD_DIM]
            values[row, :HEAD_DIM] = both[:, HEAD_DIM:]
        for i in range(ids.shape[0] - at_chosen):
            picked = ids[at_chosen + i]

            @pl.when(picked % seq_count == me ^ k)
            def _():
                row = pl.ds(pl.multiple_of((at * spans + picked // seq_count) * block, block), block)
                keys[row, :] = fresh[pl.ds(i * block, block), :HEAD_DIM]
                values[row, :HEAD_DIM] = fresh[pl.ds(i * block, block), HEAD_DIM:]

    local = lax.broadcasted_iota(jnp.int32, (quad_rows, 1), 0)
    listed = (ids[1] * KV_HEADS + (ids[2] ^ (local // rows))) * rows + local % rows
    which = listed // block
    place = jnp.zeros((quad_rows, 1), jnp.int32)
    for i in range(ids.shape[0] - at_chosen):
        place = jnp.where(which == i, ids[at_chosen + i] * block, place)
    place = place + listed % block
    for at, k in enumerate(ks):
        for j in range(spans):
            key = (j * seq_count + (me ^ k)) * block + lax.broadcasted_iota(jnp.int32, (quad_rows, block), 1)
            bias[:, pl.ds((at * spans + j) * block, block)] = jnp.where(key <= place, 0.0, LOW)

    scale = math.log2(math.e) / math.sqrt(HEAD_DIM)
    wide = stacked * quad_rows
    for h in range(0, group, stacked):
        cols = [pl.ds((h + i) * HEAD_DIM, HEAD_DIM) for i in range(stacked)]
        query = jnp.concatenate([part[:, c] for c in cols for part in q], axis=0)
        s = lax.dot_general(query, keys[...], (((1,), (1,)), ((), ())), preferred_element_type=F32)
        s = (s.reshape(stacked, quad_rows, count) * scale + bias[...][None]).reshape(wide, count)
        top = jnp.broadcast_to(jnp.max(s, axis=1, keepdims=True), (wide, HEAD_DIM))
        if not first:
            before = top_in[h // stacked]
            top = jnp.maximum(top, before)
        p = jnp.exp2(s - jnp.concatenate([top] * (count // HEAD_DIM), axis=1))
        both = jnp.dot(p.astype(BF16), values[...], preferred_element_type=F32)
        acc, total = both[:, :HEAD_DIM], both[:, HEAD_DIM:]
        if not first:
            factor = jnp.exp2(before - top)
            acc = acc + factor * acc_in[h // stacked]
            total = total + factor * total_in[h // stacked]
        if last:
            done = acc / total
            for i in range(stacked):
                for d in range(KV_HEADS):
                    at = i * quad_rows + d * rows
                    out = (outs[0], outs[1].at[0], outs[2].at[0], outs[1].at[1])[d]
                    out[:, cols[i]] = done[at : at + rows].astype(BF16)
        else:
            outs[0][h // stacked] = acc
            outs[1][h // stacked] = top
            outs[2][h // stacked] = total


def attend(ks, state, last, seq_count, rows, group, at_chosen, ids, q, fresh, messages):
    quad_rows = KV_HEADS * rows
    arrays, views = arrays_of([view for message in messages for view in message] + q)
    q_views, views = views[-len(q) :], group_views(views, messages)
    spans, block, kv_width = messages[0][0][0].shape[-3:]
    keys = len(ks) * spans * block
    stacked = 2 - group % 2
    if last:
        one = jax.ShapeDtypeStruct((rows, group * HEAD_DIM), BF16)
        out_shape = [one] + [jax.ShapeDtypeStruct((2, *one.shape), BF16)] * 2
    else:
        out_shape = [jax.ShapeDtypeStruct((group // stacked, stacked * quad_rows, HEAD_DIM), F32)] * 3
    inputs = [ids, fresh, *arrays, *(state or ())]
    return pl.pallas_call(
        functools.partial(
            attend_kernel,
            ks,
            state is None,
            last,
            seq_count,
            rows,
            stacked,
            group,
            len(arrays),
            views,
            q_views,
            at_chosen,
        ),
        out_shape=out_shape,
        in_specs=[SMEM] + [VMEM] * (len(inputs) - 1),
        out_specs=[VMEM] * len(out_shape),
        scratch_shapes=[
            pltpu.VMEM((keys, HEAD_DIM), BF16),
            pltpu.VMEM((keys, 2 * HEAD_DIM), BF16),
            pltpu.VMEM((quad_rows, keys), F32),
        ],
        compiler_params=PARAMS,
        cost_estimate=CHEAP,
        name="attend",
    )(*inputs)


def slot_of(ks, k, head):
    at = ks.index(k)
    whole = min(KV_HEADS, len(ks) - at // KV_HEADS * KV_HEADS)
    return at // KV_HEADS * KV_HEADS + ((head ^ k) & (whole - 1))


def runs_kernel(ks, seq_count, count_in, views, at_chosen, ids, fresh, *rest):
    messages, outs = [look(rest[:count_in], v) for v in views], rest[count_in:]
    spans, block, _ = messages[0][0].shape
    run = outs[0].shape[2]
    me = ids[1] * KV_HEADS + ids[2]
    slab = len(outs) * run
    offset = ids[1] * slab

    def put(k, j, source, first):
        slot = slot_of(ks, k, ids[2])
        for m, out in enumerate(outs):
            if run % 16:
                rows = source(pl.ds(pl.multiple_of(first + offset, slab), slab)).astype(F32)
                out[slot, j] = rows[m * run : (m + 1) * run].astype(BF16)
            else:
                row = first + offset + (ids[2] ^ m) * run
                out[slot, j] = source(pl.ds(pl.multiple_of(row, run), run))

    for at, k in enumerate(ks):
        for j in range(spans):
            put(k, j, arrived_of([m.at[j] for m in messages[at]], me ^ k), 0)
        for i in range(ids.shape[0] - at_chosen):
            picked = ids[at_chosen + i]

            @pl.when(picked % seq_count == me ^ k)
            def _():
                put(k, picked // seq_count, lambda rows: fresh[rows], i * block)


def cut_runs(ks, seq_count, run, heads, at_chosen, ids, fresh, messages):
    arrays, views = arrays_of([view for message in messages for view in message])
    views = group_views(views, messages)
    spans, _, kv_width = messages[0][0][0].shape[-3:]
    return pl.pallas_call(
        functools.partial(runs_kernel, ks, seq_count, len(arrays), views, at_chosen),
        out_shape=[jax.ShapeDtypeStruct((len(ks), spans, run, kv_width), BF16)] * heads,
        in_specs=[SMEM, VMEM] + [VMEM] * len(arrays),
        out_specs=[VMEM] * heads,
        compiler_params=PARAMS,
        cost_estimate=CHEAP,
        name="runs",
    )(ids, fresh, *arrays)


def finish_kernel(seq_count, views, count_in, ids, *rest):
    parts, landed, (joined, out, laid_out, sems) = look(rest[:count_in], views), rest[count_in:-4], rest[-4:]
    spans, run, width = landed[0].shape[1:]
    part_width = parts[0].shape[1]
    copies = []
    for d, part in enumerate(parts):
        cols = pl.ds(pl.multiple_of((ids[3] ^ turn(d)) * part_width, HEAD_DIM), part_width)
        copies.append(pltpu.make_async_copy(part, joined.at[0, :, cols], sems.at[0, d]))
        copies[-1].start()
    count = seq_count * spans * run
    blocks = spans * seq_count
    at = lax.broadcasted_iota(jnp.int32, (count, count), 1)
    to = lax.broadcasted_iota(jnp.int32, (count, count), 0)

    def order_of(sender):
        source = at // (spans * run)
        half = jnp.where(source < seq_count - KV_HEADS, 0, sender & KV_HEADS // 2)
        target = (at % run) * blocks + (at // run) % spans * seq_count + (ids[1] * KV_HEADS ^ source ^ half)
        return (to == target).astype(F32).astype(BF16)

    for k in range(KV_HEADS):
        if k % (KV_HEADS // 2) == 0:
            order = order_of(ids[2] ^ k)
        rows = [landed[i + k][...] for i in range(0, len(landed), KV_HEADS)]
        if run % 16:
            rows = [part.astype(F32) for part in rows]
        rows = jnp.concatenate([part.reshape(-1, width) for part in rows], axis=0).astype(BF16)
        laid = jnp.dot(order, rows, preferred_element_type=F32)
        request = ids[0] ^ turn(ids[2] ^ k)
        for u in range(run):
            laid_out[k, :, pl.ds(u * width, width)] = laid[u * blocks : (u + 1) * blocks].astype(BF16)
        copies.append(pltpu.make_async_copy(laid_out.at[k], out.at[0, 0, request], sems.at[1, k]))
        copies[-1].start()
    for copy in copies:
        copy.wait()


def shards(pool_kv, span_home, span_order, chosen, fresh_q, fresh_kv):
    pool_count, quads, heads = (lax.axis_size(a) for a in ("pool", "quad", "head"))
    seq_count = quads * heads
    me, quad, head = (lax.axis_index(a) for a in ("pool", "quad", "head"))
    slots, block, width = pool_kv.shape
    spans = span_order.shape[1]
    rows, q_width = fresh_q.shape[1:]
    kv_width = width // heads
    q_part = q_width // heads
    run = block // seq_count
    group = q_part // HEAD_DIM
    place = jnp.stack([me, quad, head, me ^ turn(head)]).astype(jnp.int32)
    ids = jnp.concatenate([place, span_home, span_order[0], chosen[0]])
    at_chosen = HOME + span_home.shape[0] + spans
    seat = quad * heads + head

    def after(value, *others):
        return lax.optimization_barrier((value, others))[0]

    def swap(value, axes, count, k):
        return lax.ppermute(value, axes, [(i, i ^ k) for i in range(count)])

    seq = ("quad", "head")
    to_pool = pl.pallas_call(
        functools.partial(pack_kernel, slots, spans),
        out_shape=[jax.ShapeDtypeStruct((block, kv_width), BF16)] * pool_count
        + [jax.ShapeDtypeStruct((block, width - kv_width), BF16)] * pool_count,
        in_specs=[SMEM, ANY],
        out_specs=[ANY] * (2 * pool_count),
        scratch_shapes=[pltpu.SemaphoreType.DMA((pool_count, heads))],
        compiler_params=PARAMS,
        cost_estimate=CHEAP,
        name="pack",
    )(ids, pool_kv)
    far = [swap(after(fresh_kv, to_pool[0]), "quad", quads, k) for k in range(1, quads)]

    def from_pool(values, out_shape, *dep):
        arrived = [values[0]] + [None] * (pool_count - 1)
        for k in reversed(range(1, pool_count)):
            arrived[k] = swap(values[k], "pool", pool_count, k)
        return pl.pallas_call(
            functools.partial(choose_kernel, slots, pool_count),
            out_shape=out_shape,
            in_specs=[SMEM] + [ANY] * pool_count,
            out_specs=[ANY] * len(out_shape),
            scratch_shapes=[pltpu.SemaphoreType.DMA((spans, heads - 1))],
            compiler_params=PARAMS,
            cost_estimate=CHEAP,
            name="choose",
        )(ids, *after(arrived, dep))

    blocks = jax.ShapeDtypeStruct((spans, block, kv_width), BF16)
    (own,) = from_pool(to_pool[:pool_count], [blocks], far)
    early = [swap(own, "quad", quads, a) for a in range(1, quads)]
    def place(got, send):
        like = jax.ShapeDtypeStruct(send.shape, BF16)
        return pl.pallas_call(
            place_kernel,
            out_shape=[jax.ShapeDtypeStruct(send.shape[1:], BF16), like],
            in_specs=[VMEM] * 2,
            out_specs=[VMEM] * 2,
            input_output_aliases={1: 1},
            compiler_params=PARAMS,
            cost_estimate=CHEAP,
            name="place",
        )(got, send)

    one = jax.ShapeDtypeStruct((rows, q_part + quads * kv_width), BF16)
    pair = jax.ShapeDtypeStruct((2, *one.shape), BF16)
    keep, give, send = pl.pallas_call(
        split_kernel,
        out_shape=[one, pair, pair],
        in_specs=[SMEM, ANY, ANY, ANY],
        out_specs=[ANY] * 3,
        scratch_shapes=[pltpu.SemaphoreType.DMA(((1 + quads) * heads,))],
        compiler_params=PARAMS,
        cost_estimate=CHEAP,
        name="split",
    )(ids, fresh_q, fresh_kv, far[0] if quads == 2 else jnp.concatenate(far, axis=0))
    chip = swap(send, "head", heads, 2)
    give = pl.pallas_call(
        follow_kernel,
        out_shape=pair,
        in_specs=[VMEM] * 2,
        out_specs=VMEM,
        input_output_aliases={1: 0},
        compiler_params=PARAMS,
        cost_estimate=CHEAP,
        name="follow",
    )(chip, give)
    core = swap(give, "head", heads, 1)
    q_give, q = give, [(keep, None), (core, 0), (chip, 0), (core, 1)]

    pair = jax.ShapeDtypeStruct((2, *blocks.shape), BF16)
    give, kv_send = from_pool(to_pool[pool_count:], [pair] * 2, send, early)
    beside, kv_send = place(after(swap(give, "head", heads, 1), q_give), kv_send)
    rest = swap(kv_send, "head", heads, 2)
    messages = [[(own, None)], [(beside, None)], [(rest, 0)], [(rest, 1)]]

    if rows % 16:
        q = [(jnp.concatenate([part if index is None else part[index] for part, index in q], axis=0), None)]
        listed = q[0][0][:, q_part:].reshape(heads, rows, quads, kv_width).transpose(2, 0, 1, 3)
        listed = listed.reshape(seq_count, rows, kv_width)
        fresh = jnp.take(listed, seat ^ jnp.arange(seq_count), axis=0).reshape(seq_count * rows, kv_width)
    else:
        arrays, views = arrays_of(q)
        fresh = pl.pallas_call(
            functools.partial(sort_kernel, quads, views),
            out_shape=jax.ShapeDtypeStruct((seq_count * rows, kv_width), BF16),
            in_specs=[SMEM] + [VMEM] * len(arrays),
            out_specs=VMEM,
            compiler_params=PARAMS,
            cost_estimate=CHEAP,
            name="sort",
        )(ids, *arrays)

    def to_decode(ks, *dep):
        parts = [messages[k] for k in ks]
        arrays, views = arrays_of([view for message in parts for view in message])
        arrays = after(arrays, dep)
        parts = group_views([(arrays[i], index) for i, index in views], parts)
        cut = cut_runs(ks, seq_count, run, heads, at_chosen, ids, fresh, parts)
        if run % 16:
            cut = [lax.dynamic_index_in_dim(jnp.stack(cut), head ^ k, axis=0, keepdims=False) for k in range(heads)]
        went = [None] * heads
        for k in reversed(range(heads)):
            perm = [
                ((r * quads + a) * heads + i, ((r ^ turn(i)) * quads + a) * heads + (i ^ k))
                for r in range(pool_count)
                for a in range(quads)
                for i in range(heads)
            ]
            went[k] = lax.ppermute(cut[k], ("pool", "quad", "head"), perm)
        return went, cut

    def work(ks, state, last=False):
        return attend(ks, state, last, seq_count, rows, group, at_chosen, ids, q, fresh, [messages[k] for k in ks])

    soons = []
    for a in range(1, quads):
        second = swap(beside, "quad", quads, a)
        messages += [[(early[a - 1], None)], [(second, None)], None, None]
    first = [0, 1, *range(heads, seq_count, heads)]
    state = None
    for at in range(0, len(first), 6):
        state = work(first[at : at + 6], state)
    firsts = [i for i in range(seq_count) if ahead(i)]
    for a in range(1, quads):
        at = a * heads
        soon = lax.ppermute(kv_send, ("quad", "head"), [(i, i ^ at ^ 2) for i in firsts])
        late = lax.ppermute(after(rest, messages[at + 1], state), ("quad", "head"), [(i, i ^ at) for i in firsts])
        messages[at + 2 : at + 4] = [[(soon, 0), (late, 0)], [(soon, 1), (late, 1)]]
        soons.append(soon)
    groups = [list(range(seq_count - 2)), [seq_count - 2, seq_count - 1]]
    second = [k for k in groups[0] if k not in first]
    landed = [to_decode(groups[0], state)]
    state = after(state, soons, landed[0][1])
    for at in range(0, len(second), 6):
        state = work(second[at : at + 6], state)
    keep, give, send = work(groups[-1], state, True)
    beside, send = place(swap(after(give, landed[0][0]), "head", heads, 1), send)
    landed.append(to_decode(groups[1], keep))
    chip = swap(send, "head", heads, 2)
    arrays, views = arrays_of([(keep, None), (beside, None), (chip, 0), (chip, 1)])
    runs = [part for went, _ in landed for part in went]
    return pl.pallas_call(
        functools.partial(finish_kernel, seq_count, views, len(arrays)),
        out_shape=[
            jax.ShapeDtypeStruct((1, rows, q_width), BF16),
            jax.ShapeDtypeStruct((1, 1, pool_count, spans * seq_count, run * kv_width), BF16),
        ],
        in_specs=[SMEM] + [VMEM] * (len(arrays) + len(runs)),
        out_specs=[ANY] * 2,
        scratch_shapes=[
            pltpu.VMEM((pool_count, spans * seq_count, run * kv_width), BF16),
            pltpu.SemaphoreType.DMA((2, max(pool_count, heads))),
        ],
        compiler_params=PARAMS,
        cost_estimate=CHEAP,
        name="finish",
    )(ids, *arrays, *runs)


def solution(mesh):
    pool_count, seq_count = mesh.shape["pool"], mesh.shape["seq"]
    fine = Mesh(mesh.devices.reshape(pool_count, seq_count // KV_HEADS, KV_HEADS), ("pool", "quad", "head"))
    seq = ("quad", "head")
    in_specs = (
        P("pool", seq, None),
        P(),
        P("pool", None),
        P("pool", None),
        P("pool", seq, None),
        P("pool", seq, None),
    )
    out_specs = (P("pool", seq, None), P("pool", seq, None, None, None))
    return jax.shard_map(shards, mesh=fine, in_specs=in_specs, out_specs=out_specs, check_vma=False)
```

```python
import functools
import math

import jax
import jax.numpy as jnp
from jax import lax
from jax.experimental import pallas as pl
from jax.experimental.pallas import tpu as pltpu
from jax.sharding import Mesh, PartitionSpec as P

KV_HEADS = 4
HEAD_DIM = 128
LOW = -1e30
HOME = 4
BF16 = jnp.bfloat16
F32 = jnp.float32

SMEM = pl.BlockSpec(memory_space=pltpu.SMEM)
VMEM = pl.BlockSpec(memory_space=pltpu.VMEM)
ANY = pl.BlockSpec(memory_space=pl.ANY)
HBM = pl.BlockSpec(memory_space=pltpu.HBM)
PARAMS = pltpu.CompilerParams(vmem_limit_bytes=40 * 1024 * 1024)
CHEAP = pl.CostEstimate(flops=1, bytes_accessed=1, transcendentals=1)
FULL = pltpu.CompilerParams(vmem_limit_bytes=60 * 1024 * 1024)


def turn(d):
    return (d & 1) * 3 ^ d >> 1


def pack_kernel(slots, spans, ids, pool_kv, *rest):
    pool_count = (len(rest) - 1) // 2
    first, others, sems = rest[:pool_count], rest[pool_count:-1], rest[-1]
    width = first[0].shape[1]
    copies = []
    for d in range(pool_count):
        slot = jnp.int32(0)
        for t in range(spans):
            held = ids[HOME + (ids[0] ^ d) * spans + t]
            slot = jnp.where(held // slots == ids[0], held % slots, slot)
        for n in range(KV_HEADS):
            source = pool_kv.at[slot, :, pl.ds(pl.multiple_of((ids[3] ^ d ^ turn(n)) * width, HEAD_DIM), width)]
            out = others[d].at[:, pl.ds((n - 1) * width, width)] if n else first[d]
            copies.append(pltpu.make_async_copy(source, out, sems.at[d, n]))
            copies[-1].start()
    for copy in copies:
        copy.wait()


def split_kernel(ids, fresh_q, near, far, *rest):
    keep, give, send, sems = rest
    outs = (keep, give.at[0], send.at[0], send.at[1])
    q_width = fresh_q.shape[2] // KV_HEADS
    kv_width = near.shape[2] // KV_HEADS
    copies = []

    def copy(source, out, at):
        copies.append(pltpu.make_async_copy(source, out.at[:, at], sems.at[len(copies)]))
        copies[-1].start()

    for d, out in enumerate(outs):
        other = ids[3] ^ turn(d)
        q_at = pl.ds(pl.multiple_of(other * q_width, HEAD_DIM), q_width)
        kv_at = pl.ds(pl.multiple_of(other * kv_width, HEAD_DIM), kv_width)
        copy(fresh_q.at[0, :, q_at], out, pl.ds(0, q_width))
        copy(near.at[0, :, kv_at], out, pl.ds(q_width, kv_width))
        for a in range(far.shape[0]):
            copy(far.at[a, :, kv_at], out, pl.ds(q_width + (a + 1) * kv_width, kv_width))
    for each in copies:
        each.wait()


def arrays_of(views):
    arrays = []
    for array, _ in views:
        if not any(array is a for a in arrays):
            arrays.append(array)
    return arrays, [(next(i for i, a in enumerate(arrays) if a is array), index) for array, index in views]


def look(refs, views):
    return [refs[i] if index is None else refs[i].at[index] for i, index in views]


def ahead(seat):
    return (seat // (KV_HEADS // 2) ^ seat // KV_HEADS) & 1


def arrived_of(refs, seat):
    if len(refs) == 1:
        return lambda at: refs[0][at]
    return lambda at: jnp.where(ahead(seat) == 1, refs[0][at], refs[1][at])


def group_views(views, messages):
    views = iter(views)
    return [[next(views) for _ in message] for message in messages]


def sort_kernel(quads, views, ids, *rest):
    parts, out = look(rest[:-1], views), rest[-1]
    rows, width = parts[0].shape[0], out.shape[1]
    for d, part in enumerate(parts):
        for a in range(quads):
            seat = (ids[1] ^ a) * KV_HEADS + (ids[2] ^ d)
            first = part.shape[1] - (quads - a) * width
            out[pl.ds(pl.multiple_of(seat * rows, rows), rows), :] = part[:, first : first + width]


def choose_kernel(slots, pool_count, ids, *rest):
    arrived, outs, sems = rest[:pool_count], rest[pool_count:-1], rest[-1]
    if len(outs) == 2:
        give, send = outs
        outs = (give.at[0], send.at[0], give.at[1])
    spans = sems.shape[0]
    width = outs[0].shape[2]
    for start in (True, False):
        for j in range(spans):
            source = (ids[HOME + ids[HOME + pool_count * spans + j]] // slots) ^ ids[0]
            for n, out in enumerate(outs):
                at = pl.ds(n * width, width)
                if start:
                    for p in range(pool_count):

                        @pl.when(source == p)
                        def _(p=p):
                            pltpu.make_async_copy(arrived[p].at[:, at], out.at[j], sems.at[j, n]).start()

                else:
                    pltpu.make_async_copy(arrived[0].at[:, at], out.at[j], sems.at[j, n]).wait()


def place_kernel(got, send_in, beside, send):
    del send_in
    beside[...] = got[0]
    send[1] = got[1]


def follow_kernel(got, give_in, give):
    del give_in
    give[1] = got[1]


def attend_kernel(ks, first, last, seq_count, rows, stacked, group, count_in, views, q_views, at_chosen, ids, fresh, *rest):
    messages, q = [look(rest[:count_in], v) for v in views], look(rest[:count_in], q_views)
    rest = rest[count_in:]
    spans, block, _ = messages[0][0].shape
    quad_rows = KV_HEADS * rows
    if not first:
        (acc_in, top_in, total_in), rest = rest[:3], rest[3:]
    outs, (keys, values, bias) = rest[:-3], rest[-3:]
    count = keys.shape[0]
    me = ids[1] * KV_HEADS + ids[2]

    values[:, HEAD_DIM:] = jnp.ones((count, HEAD_DIM), BF16)
    for at, k in enumerate(ks):
        for j in range(spans):
            row = pl.ds((at * spans + j) * block, block)
            both = arrived_of(messages[at], me ^ k)(j)
            keys[row, :] = both[:, :HEAD_DIM]
            values[row, :HEAD_DIM] = both[:, HEAD_DIM:]
        for i in range(ids.shape[0] - at_chosen):
            picked = ids[at_chosen + i]

            @pl.when(picked % seq_count == me ^ k)
            def _():
                row = pl.ds(pl.multiple_of((at * spans + picked // seq_count) * block, block), block)
                keys[row, :] = fresh[pl.ds(i * block, block), :HEAD_DIM]
                values[row, :HEAD_DIM] = fresh[pl.ds(i * block, block), HEAD_DIM:]

    local = lax.broadcasted_iota(jnp.int32, (quad_rows, 1), 0)
    listed = (ids[1] * KV_HEADS + (ids[2] ^ (local // rows))) * rows + local % rows
    which = listed // block
    place = jnp.zeros((quad_rows, 1), jnp.int32)
    for i in range(ids.shape[0] - at_chosen):
        place = jnp.where(which == i, ids[at_chosen + i] * block, place)
    place = place + listed % block
    for at, k in enumerate(ks):
        for j in range(spans):
            key = (j * seq_count + (me ^ k)) * block + lax.broadcasted_iota(jnp.int32, (quad_rows, block), 1)
            bias[:, pl.ds((at * spans + j) * block, block)] = jnp.where(key <= place, 0.0, LOW)

    scale = math.log2(math.e) / math.sqrt(HEAD_DIM)
    wide = stacked * quad_rows
    for h in range(0, group, stacked):
        cols = [pl.ds((h + i) * HEAD_DIM, HEAD_DIM) for i in range(stacked)]
        query = jnp.concatenate([part[:, c] for c in cols for part in q], axis=0)
        s = lax.dot_general(query, keys[...], (((1,), (1,)), ((), ())), preferred_element_type=F32)
        s = (s.reshape(stacked, quad_rows, count) * scale + bias[...][None]).reshape(wide, count)
        top = jnp.broadcast_to(jnp.max(s, axis=1, keepdims=True), (wide, HEAD_DIM))
        if not first:
            before = top_in[h // stacked]
            top = jnp.maximum(top, before)
        p = jnp.exp2(s - jnp.concatenate([top] * (count // HEAD_DIM), axis=1))
        both = jnp.dot(p.astype(BF16), values[...], preferred_element_type=F32)
        acc, total = both[:, :HEAD_DIM], both[:, HEAD_DIM:]
        if not first:
            factor = jnp.exp2(before - top)
            acc = acc + factor * acc_in[h // stacked]
            total = total + factor * total_in[h // stacked]
        if last:
            done = acc / total
            for i in range(stacked):
                for d in range(KV_HEADS):
                    at = i * quad_rows + d * rows
                    out = (outs[0], outs[1].at[0], outs[2].at[0], outs[1].at[1])[d]
                    out[:, cols[i]] = done[at : at + rows].astype(BF16)
        else:
            outs[0][h // stacked] = acc
            outs[1][h // stacked] = top
            outs[2][h // stacked] = total


def attend(ks, state, last, seq_count, rows, group, at_chosen, ids, q, fresh, messages):
    quad_rows = KV_HEADS * rows
    arrays, views = arrays_of([view for message in messages for view in message] + q)
    q_views, views = views[-len(q) :], group_views(views, messages)
    spans, block, kv_width = messages[0][0][0].shape[-3:]
    keys = len(ks) * spans * block
    stacked = 2 - group % 2
    if last:
        one = jax.ShapeDtypeStruct((rows, group * HEAD_DIM), BF16)
        out_shape = [one] + [jax.ShapeDtypeStruct((2, *one.shape), BF16)] * 2
    else:
        out_shape = [jax.ShapeDtypeStruct((group // stacked, stacked * quad_rows, HEAD_DIM), F32)] * 3
    inputs = [ids, fresh, *arrays, *(state or ())]
    return pl.pallas_call(
        functools.partial(
            attend_kernel,
            ks,
            state is None,
            last,
            seq_count,
            rows,
            stacked,
            group,
            len(arrays),
            views,
            q_views,
            at_chosen,
        ),
        out_shape=out_shape,
        in_specs=[SMEM] + [VMEM] * (len(inputs) - 1),
        out_specs=[VMEM] * len(out_shape),
        scratch_shapes=[
            pltpu.VMEM((keys, HEAD_DIM), BF16),
            pltpu.VMEM((keys, 2 * HEAD_DIM), BF16),
            pltpu.VMEM((quad_rows, keys), F32),
        ],
        compiler_params=PARAMS,
        cost_estimate=CHEAP,
        name="attend",
    )(*inputs)


def slot_of(ks, k, head):
    at = ks.index(k)
    whole = min(KV_HEADS, len(ks) - at // KV_HEADS * KV_HEADS)
    return at // KV_HEADS * KV_HEADS + ((head ^ k) & (whole - 1))


def runs_kernel(ks, turned, seq_count, count_in, views, at_chosen, ids, fresh, *rest):
    messages, outs = [look(rest[:count_in], v) for v in views], rest[count_in:]
    spans, block, _ = messages[0][0].shape
    run = outs[0].shape[2]
    me = ids[1] * KV_HEADS + ids[2]
    slab = len(outs) * run
    offset = ids[1] * slab

    def put(k, j, source, first):
        slot = slot_of(ks, k, ids[2])
        for m, out in enumerate(outs):
            if run % 16:
                rows = source(pl.ds(pl.multiple_of(first + offset, slab), slab)).astype(F32)
                out[slot, j] = rows[m * run : (m + 1) * run].astype(BF16)
            else:
                row = first + offset + (ids[2] ^ m ^ turned) * run
                out[slot, j] = source(pl.ds(pl.multiple_of(row, run), run))

    for at, k in enumerate(ks):
        for j in range(spans):
            put(k, j, arrived_of([m.at[j] for m in messages[at]], me ^ k), 0)
        for i in range(ids.shape[0] - at_chosen):
            picked = ids[at_chosen + i]

            @pl.when(picked % seq_count == me ^ k)
            def _():
                put(k, picked // seq_count, lambda rows: fresh[rows], i * block)


def cut_runs(ks, turned, seq_count, run, heads, at_chosen, ids, fresh, messages):
    arrays, views = arrays_of([view for message in messages for view in message])
    views = group_views(views, messages)
    spans, _, kv_width = messages[0][0][0].shape[-3:]
    return pl.pallas_call(
        functools.partial(runs_kernel, ks, turned, seq_count, len(arrays), views, at_chosen),
        out_shape=[jax.ShapeDtypeStruct((len(ks), spans, run, kv_width), BF16)] * heads,
        in_specs=[SMEM, VMEM] + [VMEM] * len(arrays),
        out_specs=[VMEM] * heads,
        compiler_params=PARAMS,
        cost_estimate=CHEAP,
        name="runs",
    )(ids, fresh, *arrays)


def finish_kernel(seq_count, views, count_in, ids, *rest):
    parts, landed, (joined, out, laid_out, sems) = look(rest[:count_in], views), rest[count_in:-4], rest[-4:]
    spans, run, width = landed[0].shape[1:]
    part_width = parts[0].shape[1]
    copies = []
    for d, part in enumerate(parts):
        cols = pl.ds(pl.multiple_of((ids[3] ^ turn(d)) * part_width, HEAD_DIM), part_width)
        copies.append(pltpu.make_async_copy(part, joined.at[0, :, cols], sems.at[0, d]))
        copies[-1].start()
    count = seq_count * spans * run
    blocks = spans * seq_count
    at = lax.broadcasted_iota(jnp.int32, (count, count), 1)
    to = lax.broadcasted_iota(jnp.int32, (count, count), 0)

    def order_of(sender):
        source = at // (spans * run)
        half = jnp.where(source < seq_count - KV_HEADS, 0, sender & KV_HEADS // 2)
        target = (at % run) * blocks + (at // run) % spans * seq_count + (ids[1] * KV_HEADS ^ source ^ half)
        return (to == target).astype(F32).astype(BF16)

    for k in range(KV_HEADS):
        if k % (KV_HEADS // 2) == 0:
            order = order_of(ids[2] ^ k)
        rows = [landed[i + k][...] for i in range(0, len(landed), KV_HEADS)]
        if run % 16:
            rows = [part.astype(F32) for part in rows]
        rows = jnp.concatenate([part.reshape(-1, width) for part in rows], axis=0).astype(BF16)
        laid = jnp.dot(order, rows, preferred_element_type=F32)
        request = ids[0] ^ turn(ids[2] ^ k)
        for u in range(run):
            laid_out[k, :, pl.ds(u * width, width)] = laid[u * blocks : (u + 1) * blocks].astype(BF16)
        copies.append(pltpu.make_async_copy(laid_out.at[k], out.at[0, 0, request], sems.at[1, k]))
        copies[-1].start()
    for copy in copies:
        copy.wait()


def shards(pool_kv, span_home, span_order, chosen, fresh_q, fresh_kv):
    pool_count, quads, heads = (lax.axis_size(a) for a in ("pool", "quad", "head"))
    seq_count = quads * heads
    me, quad, head = (lax.axis_index(a) for a in ("pool", "quad", "head"))
    slots, block, width = pool_kv.shape
    spans = span_order.shape[1]
    rows, q_width = fresh_q.shape[1:]
    kv_width = width // heads
    q_part = q_width // heads
    run = block // seq_count
    group = q_part // HEAD_DIM
    place = jnp.stack([me, quad, head, me ^ turn(head)]).astype(jnp.int32)
    ids = jnp.concatenate([place, span_home, span_order[0], chosen[0]])
    at_chosen = HOME + span_home.shape[0] + spans
    seat = quad * heads + head

    def after(value, *others):
        return lax.optimization_barrier((value, others))[0]

    def swap(value, axes, count, k):
        return lax.ppermute(value, axes, [(i, i ^ k) for i in range(count)])

    seq = ("quad", "head")
    to_pool = pl.pallas_call(
        functools.partial(pack_kernel, slots, spans),
        out_shape=[jax.ShapeDtypeStruct((block, kv_width), BF16)] * pool_count
        + [jax.ShapeDtypeStruct((block, width - kv_width), BF16)] * pool_count,
        in_specs=[SMEM, ANY],
        out_specs=[ANY] * (2 * pool_count),
        scratch_shapes=[pltpu.SemaphoreType.DMA((pool_count, heads))],
        compiler_params=PARAMS,
        cost_estimate=CHEAP,
        name="pack",
    )(ids, pool_kv)
    far = [swap(after(fresh_kv, to_pool[0]), "quad", quads, k) for k in range(1, quads)]

    def from_pool(values, out_shape, *dep):
        arrived = [values[0]] + [None] * (pool_count - 1)
        for k in reversed(range(1, pool_count)):
            arrived[k] = swap(values[k], "pool", pool_count, k)
        return pl.pallas_call(
            functools.partial(choose_kernel, slots, pool_count),
            out_shape=out_shape,
            in_specs=[SMEM] + [ANY] * pool_count,
            out_specs=[ANY] * len(out_shape),
            scratch_shapes=[pltpu.SemaphoreType.DMA((spans, heads - 1))],
            compiler_params=PARAMS,
            cost_estimate=CHEAP,
            name="choose",
        )(ids, *after(arrived, dep))

    blocks = jax.ShapeDtypeStruct((spans, block, kv_width), BF16)
    (own,) = from_pool(to_pool[:pool_count], [blocks], far)
    early = [swap(own, "quad", quads, a) for a in range(1, quads)]
    def place(got, send):
        like = jax.ShapeDtypeStruct(send.shape, BF16)
        return pl.pallas_call(
            place_kernel,
            out_shape=[jax.ShapeDtypeStruct(send.shape[1:], BF16), like],
            in_specs=[VMEM] * 2,
            out_specs=[VMEM] * 2,
            input_output_aliases={1: 1},
            compiler_params=PARAMS,
            cost_estimate=CHEAP,
            name="place",
        )(got, send)

    one = jax.ShapeDtypeStruct((rows, q_part + quads * kv_width), BF16)
    pair = jax.ShapeDtypeStruct((2, *one.shape), BF16)
    keep, give, send = pl.pallas_call(
        split_kernel,
        out_shape=[one, pair, pair],
        in_specs=[SMEM, ANY, ANY, ANY],
        out_specs=[ANY] * 3,
        scratch_shapes=[pltpu.SemaphoreType.DMA(((1 + quads) * heads,))],
        compiler_params=PARAMS,
        cost_estimate=CHEAP,
        name="split",
    )(ids, fresh_q, fresh_kv, far[0] if quads == 2 else jnp.concatenate(far, axis=0))
    chip = swap(send, "head", heads, 2)
    give = pl.pallas_call(
        follow_kernel,
        out_shape=pair,
        in_specs=[VMEM] * 2,
        out_specs=VMEM,
        input_output_aliases={1: 0},
        compiler_params=PARAMS,
        cost_estimate=CHEAP,
        name="follow",
    )(chip, give)
    core = swap(give, "head", heads, 1)
    q_give, q = give, [(keep, None), (core, 0), (chip, 0), (core, 1)]

    pair = jax.ShapeDtypeStruct((2, *blocks.shape), BF16)
    give, kv_send = from_pool(to_pool[pool_count:], [pair] * 2, send, early)
    beside, kv_send = place(after(swap(give, "head", heads, 1), q_give), kv_send)
    rest = swap(kv_send, "head", heads, 2)
    messages = [[(own, None)], [(beside, None)], [(rest, 0)], [(rest, 1)]]

    if rows % 16:
        q = [(jnp.concatenate([part if index is None else part[index] for part, index in q], axis=0), None)]
        listed = q[0][0][:, q_part:].reshape(heads, rows, quads, kv_width).transpose(2, 0, 1, 3)
        listed = listed.reshape(seq_count, rows, kv_width)
        fresh = jnp.take(listed, seat ^ jnp.arange(seq_count), axis=0).reshape(seq_count * rows, kv_width)
    else:
        arrays, views = arrays_of(q)
        fresh = pl.pallas_call(
            functools.partial(sort_kernel, quads, views),
            out_shape=jax.ShapeDtypeStruct((seq_count * rows, kv_width), BF16),
            in_specs=[SMEM] + [VMEM] * len(arrays),
            out_specs=VMEM,
            compiler_params=PARAMS,
            cost_estimate=CHEAP,
            name="sort",
        )(ids, *arrays)

    def to_decode(ks, turned, *dep):
        parts = [messages[k] for k in ks]
        arrays, views = arrays_of([view for message in parts for view in message])
        arrays = after(arrays, dep)
        parts = group_views([(arrays[i], index) for i, index in views], parts)
        cut = cut_runs(ks, turned, seq_count, run, heads, at_chosen, ids, fresh, parts)
        if run % 16:
            cut = [lax.dynamic_index_in_dim(jnp.stack(cut), head ^ k ^ turned, axis=0, keepdims=False) for k in range(heads)]
        went = [None] * heads
        for k in reversed(range(heads)):
            perm = [
                ((r * quads + a) * heads + i, ((r ^ turn(i)) * quads + a) * heads + (i ^ k ^ turned))
                for r in range(pool_count)
                for a in range(quads)
                for i in range(heads)
            ]
            went[k] = lax.ppermute(cut[k], ("pool", "quad", "head"), perm)
        return [went[k ^ turned] for k in range(heads)], cut

    def work(ks, state, last=False):
        return attend(ks, state, last, seq_count, rows, group, at_chosen, ids, q, fresh, [messages[k] for k in ks])

    soons = []
    for a in range(1, quads):
        second = swap(beside, "quad", quads, a)
        messages += [[(early[a - 1], None)], [(second, None)], None, None]
    first = [0, 1, *range(heads, seq_count, heads)]
    state = None
    for at in range(0, len(first), 6):
        state = work(first[at : at + 6], state)
    firsts = [i for i in range(seq_count) if ahead(i)]
    for a in range(1, quads):
        at = a * heads
        soon = lax.ppermute(kv_send, ("quad", "head"), [(i, i ^ at ^ 2) for i in firsts])
        late = lax.ppermute(after(rest, messages[at + 1], state), ("quad", "head"), [(i, i ^ at) for i in firsts])
        messages[at + 2 : at + 4] = [[(soon, 0), (late, 0)], [(soon, 1), (late, 1)]]
        soons.append(soon)
    groups = [list(range(seq_count - 2)), [seq_count - 2, seq_count - 1]]
    second = [k for k in groups[0] if k not in first]
    landed = [to_decode(groups[0], 0, state)]
    state = after(state, soons, landed[0][1])
    for at in range(0, len(second), 6):
        state = work(second[at : at + 6], state)
    keep, give, send = work(groups[-1], state, True)
    beside, send = place(swap(after(give, landed[0][0]), "head", heads, 1), send)
    landed.append(to_decode(groups[1], heads - 1, keep))
    chip = swap(send, "head", heads, 2)
    arrays, views = arrays_of([(keep, None), (beside, None), (chip, 0), (chip, 1)])
    runs = [part for went, _ in landed for part in went]
    return pl.pallas_call(
        functools.partial(finish_kernel, seq_count, views, len(arrays)),
        out_shape=[
            jax.ShapeDtypeStruct((1, rows, q_width), BF16),
            jax.ShapeDtypeStruct((1, 1, pool_count, spans * seq_count, run * kv_width), BF16),
        ],
        in_specs=[SMEM] + [VMEM] * (len(arrays) + len(runs)),
        out_specs=[ANY] * 2,
        scratch_shapes=[
            pltpu.VMEM((pool_count, spans * seq_count, run * kv_width), BF16),
            pltpu.SemaphoreType.DMA((2, max(pool_count, heads))),
        ],
        compiler_params=PARAMS,
        cost_estimate=CHEAP,
        name="finish",
    )(ids, *arrays, *runs)


def solution(mesh):
    pool_count, seq_count = mesh.shape["pool"], mesh.shape["seq"]
    fine = Mesh(mesh.devices.reshape(pool_count, seq_count // KV_HEADS, KV_HEADS), ("pool", "quad", "head"))
    seq = ("quad", "head")
    in_specs = (
        P("pool", seq, None),
        P(),
        P("pool", None),
        P("pool", None),
        P("pool", seq, None),
        P("pool", seq, None),
    )
    out_specs = (P("pool", seq, None), P("pool", seq, None, None, None))
    return jax.shard_map(shards, mesh=fine, in_specs=in_specs, out_specs=out_specs, check_vma=False)
```

```python
import functools
import math

import jax
import jax.numpy as jnp
from jax import lax
from jax.experimental import pallas as pl
from jax.experimental.pallas import tpu as pltpu
from jax.sharding import Mesh, PartitionSpec as P

KV_HEADS = 4
HEAD_DIM = 128
LOW = -1e30
HOME = 4
BF16 = jnp.bfloat16
F32 = jnp.float32

SMEM = pl.BlockSpec(memory_space=pltpu.SMEM)
VMEM = pl.BlockSpec(memory_space=pltpu.VMEM)
ANY = pl.BlockSpec(memory_space=pl.ANY)
HBM = pl.BlockSpec(memory_space=pltpu.HBM)
PARAMS = pltpu.CompilerParams(vmem_limit_bytes=40 * 1024 * 1024)
CHEAP = pl.CostEstimate(flops=1, bytes_accessed=1, transcendentals=1)
FULL = pltpu.CompilerParams(vmem_limit_bytes=60 * 1024 * 1024)


def turn(d):
    return (d & 1) * 3 ^ d >> 1


def pack_kernel(slots, spans, ids, pool_kv, *rest):
    pool_count = (len(rest) - 1) // 2
    first, others, sems = rest[:pool_count], rest[pool_count:-1], rest[-1]
    width = first[0].shape[1]
    copies = []
    for d in range(pool_count):
        slot = jnp.int32(0)
        for t in range(spans):
            held = ids[HOME + (ids[0] ^ d) * spans + t]
            slot = jnp.where(held // slots == ids[0], held % slots, slot)
        for n in range(KV_HEADS):
            source = pool_kv.at[slot, :, pl.ds(pl.multiple_of((ids[3] ^ d ^ turn(n)) * width, HEAD_DIM), width)]
            out = others[d].at[:, pl.ds((n - 1) * width, width)] if n else first[d]
            copies.append(pltpu.make_async_copy(source, out, sems.at[d, n]))
            copies[-1].start()
    for copy in copies:
        copy.wait()


def split_kernel(ids, fresh_q, near, far, *rest):
    keep, give, send, sems = rest
    outs = (keep, give.at[0], send.at[0], send.at[1])
    q_width = fresh_q.shape[2] // KV_HEADS
    kv_width = near.shape[2] // KV_HEADS
    copies = []

    def copy(source, out, at):
        copies.append(pltpu.make_async_copy(source, out.at[:, at], sems.at[len(copies)]))
        copies[-1].start()

    for d, out in enumerate(outs):
        other = ids[3] ^ turn(d)
        q_at = pl.ds(pl.multiple_of(other * q_width, HEAD_DIM), q_width)
        kv_at = pl.ds(pl.multiple_of(other * kv_width, HEAD_DIM), kv_width)
        copy(fresh_q.at[0, :, q_at], out, pl.ds(0, q_width))
        copy(near.at[0, :, kv_at], out, pl.ds(q_width, kv_width))
        for a in range(far.shape[0]):
            copy(far.at[a, :, kv_at], out, pl.ds(q_width + (a + 1) * kv_width, kv_width))
    for each in copies:
        each.wait()


def arrays_of(views):
    arrays = []
    for array, _ in views:
        if not any(array is a for a in arrays):
            arrays.append(array)
    return arrays, [(next(i for i, a in enumerate(arrays) if a is array), index) for array, index in views]


def look(refs, views):
    return [refs[i] if index is None else refs[i].at[index] for i, index in views]


def ahead(seat):
    return (seat // (KV_HEADS // 2) ^ seat // KV_HEADS) & 1


def arrived_of(refs, seat):
    if len(refs) == 1:
        return lambda at: refs[0][at]
    return lambda at: jnp.where(ahead(seat) == 1, refs[0][at], refs[1][at])


def group_views(views, messages):
    views = iter(views)
    return [[next(views) for _ in message] for message in messages]


def sort_kernel(quads, views, ids, *rest):
    parts, out = look(rest[:-1], views), rest[-1]
    rows, width = parts[0].shape[0], out.shape[1]
    for d, part in enumerate(parts):
        for a in range(quads):
            seat = (ids[1] ^ a) * KV_HEADS + (ids[2] ^ d)
            first = part.shape[1] - (quads - a) * width
            out[pl.ds(pl.multiple_of(seat * rows, rows), rows), :] = part[:, first : first + width]


def choose_kernel(slots, pool_count, ids, *rest):
    arrived, outs, sems = rest[:pool_count], rest[pool_count:-1], rest[-1]
    if len(outs) == 2:
        give, send = outs
        outs = (give.at[0], send.at[0], give.at[1])
    spans = sems.shape[0]
    width = outs[0].shape[2]
    for start in (True, False):
        for j in range(spans):
            source = (ids[HOME + ids[HOME + pool_count * spans + j]] // slots) ^ ids[0]
            for n, out in enumerate(outs):
                at = pl.ds(n * width, width)
                if start:
                    for p in range(pool_count):

                        @pl.when(source == p)
                        def _(p=p):
                            pltpu.make_async_copy(arrived[p].at[:, at], out.at[j], sems.at[j, n]).start()

                else:
                    pltpu.make_async_copy(arrived[0].at[:, at], out.at[j], sems.at[j, n]).wait()


def place_kernel(got, send_in, beside, send):
    del send_in
    beside[...] = got[0]
    send[1] = got[1]


def follow_kernel(got, give_in, give):
    del give_in
    give[1] = got[1]


def attend_kernel(ks, first, last, seq_count, rows, stacked, group, count_in, views, q_views, at_chosen, ids, fresh, *rest):
    messages, q = [look(rest[:count_in], v) for v in views], look(rest[:count_in], q_views)
    rest = rest[count_in:]
    spans, block, _ = messages[0][0].shape
    quad_rows = KV_HEADS * rows
    if not first:
        (acc_in, top_in, total_in), rest = rest[:3], rest[3:]
    outs, (keys, values, bias) = rest[:-3], rest[-3:]
    count = keys.shape[0]
    me = ids[1] * KV_HEADS + ids[2]

    values[:, HEAD_DIM:] = jnp.ones((count, HEAD_DIM), BF16)
    for at, k in enumerate(ks):
        for j in range(spans):
            row = pl.ds((at * spans + j) * block, block)
            both = arrived_of(messages[at], me ^ k)(j)
            keys[row, :] = both[:, :HEAD_DIM]
            values[row, :HEAD_DIM] = both[:, HEAD_DIM:]
        for i in range(ids.shape[0] - at_chosen):
            picked = ids[at_chosen + i]

            @pl.when(picked % seq_count == me ^ k)
            def _():
                row = pl.ds(pl.multiple_of((at * spans + picked // seq_count) * block, block), block)
                keys[row, :] = fresh[pl.ds(i * block, block), :HEAD_DIM]
                values[row, :HEAD_DIM] = fresh[pl.ds(i * block, block), HEAD_DIM:]

    local = lax.broadcasted_iota(jnp.int32, (quad_rows, 1), 0)
    listed = (ids[1] * KV_HEADS + (ids[2] ^ (local // rows))) * rows + local % rows
    which = listed // block
    place = jnp.zeros((quad_rows, 1), jnp.int32)
    for i in range(ids.shape[0] - at_chosen):
        place = jnp.where(which == i, ids[at_chosen + i] * block, place)
    place = place + listed % block
    for at, k in enumerate(ks):
        for j in range(spans):
            key = (j * seq_count + (me ^ k)) * block + lax.broadcasted_iota(jnp.int32, (quad_rows, block), 1)
            bias[:, pl.ds((at * spans + j) * block, block)] = jnp.where(key <= place, 0.0, LOW)

    scale = math.log2(math.e) / math.sqrt(HEAD_DIM)
    wide = stacked * quad_rows
    for h in range(0, group, stacked):
        cols = [pl.ds((h + i) * HEAD_DIM, HEAD_DIM) for i in range(stacked)]
        query = jnp.concatenate([part[:, c] for c in cols for part in q], axis=0)
        s = lax.dot_general(query, keys[...], (((1,), (1,)), ((), ())), preferred_element_type=F32)
        s = (s.reshape(stacked, quad_rows, count) * scale + bias[...][None]).reshape(wide, count)
        top = jnp.broadcast_to(jnp.max(s, axis=1, keepdims=True), (wide, HEAD_DIM))
        if not first:
            before = top_in[h // stacked]
            top = jnp.maximum(top, before)
        p = jnp.exp2(s - jnp.concatenate([top] * (count // HEAD_DIM), axis=1))
        both = jnp.dot(p.astype(BF16), values[...], preferred_element_type=F32)
        acc, total = both[:, :HEAD_DIM], both[:, HEAD_DIM:]
        if not first:
            factor = jnp.exp2(before - top)
            acc = acc + factor * acc_in[h // stacked]
            total = total + factor * total_in[h // stacked]
        if last:
            done = acc / total
            for i in range(stacked):
                for d in range(KV_HEADS):
                    at = i * quad_rows + d * rows
                    out = (outs[0], outs[1].at[0], outs[2].at[0], outs[1].at[1])[d]
                    out[:, cols[i]] = done[at : at + rows].astype(BF16)
        else:
            outs[0][h // stacked] = acc
            outs[1][h // stacked] = top
            outs[2][h // stacked] = total


def attend(ks, state, last, seq_count, rows, group, at_chosen, ids, q, fresh, messages):
    quad_rows = KV_HEADS * rows
    arrays, views = arrays_of([view for message in messages for view in message] + q)
    q_views, views = views[-len(q) :], group_views(views, messages)
    spans, block, kv_width = messages[0][0][0].shape[-3:]
    keys = len(ks) * spans * block
    stacked = 2 - group % 2
    if last:
        one = jax.ShapeDtypeStruct((rows, group * HEAD_DIM), BF16)
        out_shape = [one] + [jax.ShapeDtypeStruct((2, *one.shape), BF16)] * 2
    else:
        out_shape = [jax.ShapeDtypeStruct((group // stacked, stacked * quad_rows, HEAD_DIM), F32)] * 3
    inputs = [ids, fresh, *arrays, *(state or ())]
    return pl.pallas_call(
        functools.partial(
            attend_kernel,
            ks,
            state is None,
            last,
            seq_count,
            rows,
            stacked,
            group,
            len(arrays),
            views,
            q_views,
            at_chosen,
        ),
        out_shape=out_shape,
        in_specs=[SMEM] + [VMEM] * (len(inputs) - 1),
        out_specs=[VMEM] * len(out_shape),
        scratch_shapes=[
            pltpu.VMEM((keys, HEAD_DIM), BF16),
            pltpu.VMEM((keys, 2 * HEAD_DIM), BF16),
            pltpu.VMEM((quad_rows, keys), F32),
        ],
        compiler_params=PARAMS,
        cost_estimate=CHEAP,
        name="attend",
    )(*inputs)


def slot_of(ks, k, head):
    at = ks.index(k)
    whole = min(KV_HEADS, len(ks) - at // KV_HEADS * KV_HEADS)
    return at // KV_HEADS * KV_HEADS + ((head ^ k) & (whole - 1))


def runs_kernel(ks, seq_count, count_in, views, at_chosen, ids, fresh, *rest):
    messages, outs = [look(rest[:count_in], v) for v in views], rest[count_in:]
    spans, block, _ = messages[0][0].shape
    run = outs[0].shape[2]
    me = ids[1] * KV_HEADS + ids[2]
    slab = len(outs) * run
    offset = ids[1] * slab

    def put(k, j, source, first):
        slot = slot_of(ks, k, ids[2])
        for m, out in enumerate(outs):
            if run % 16:
                rows = source(pl.ds(pl.multiple_of(first + offset, slab), slab)).astype(F32)
                out[slot, j] = rows[m * run : (m + 1) * run].astype(BF16)
            else:
                row = first + offset + (ids[2] ^ m) * run
                out[slot, j] = source(pl.ds(pl.multiple_of(row, run), run))

    for at, k in enumerate(ks):
        for j in range(spans):
            put(k, j, arrived_of([m.at[j] for m in messages[at]], me ^ k), 0)
        for i in range(ids.shape[0] - at_chosen):
            picked = ids[at_chosen + i]

            @pl.when(picked % seq_count == me ^ k)
            def _():
                put(k, picked // seq_count, lambda rows: fresh[rows], i * block)


def cut_runs(ks, seq_count, run, heads, at_chosen, ids, fresh, messages):
    arrays, views = arrays_of([view for message in messages for view in message])
    views = group_views(views, messages)
    spans, _, kv_width = messages[0][0][0].shape[-3:]
    return pl.pallas_call(
        functools.partial(runs_kernel, ks, seq_count, len(arrays), views, at_chosen),
        out_shape=[jax.ShapeDtypeStruct((len(ks), spans, run, kv_width), BF16)] * heads,
        in_specs=[SMEM, VMEM] + [VMEM] * len(arrays),
        out_specs=[VMEM] * heads,
        compiler_params=PARAMS,
        cost_estimate=CHEAP,
        name="runs",
    )(ids, fresh, *arrays)


def finish_kernel(seq_count, views, count_in, ids, *rest):
    parts, landed, (joined, out, laid_out, sems) = look(rest[:count_in], views), rest[count_in:-4], rest[-4:]
    spans, run, width = landed[0].shape[1:]
    part_width = parts[0].shape[1]
    copies = []
    for d, part in enumerate(parts):
        cols = pl.ds(pl.multiple_of((ids[3] ^ turn(d)) * part_width, HEAD_DIM), part_width)
        copies.append(pltpu.make_async_copy(part, joined.at[0, :, cols], sems.at[0, d]))
        copies[-1].start()
    count = seq_count * spans * run
    blocks = spans * seq_count
    at = lax.broadcasted_iota(jnp.int32, (count, count), 1)
    to = lax.broadcasted_iota(jnp.int32, (count, count), 0)

    def order_of(sender):
        source = at // (spans * run)
        half = jnp.where(source < seq_count - KV_HEADS, 0, sender & KV_HEADS // 2)
        target = (at % run) * blocks + (at // run) % spans * seq_count + (ids[1] * KV_HEADS ^ source ^ half)
        return (to == target).astype(F32).astype(BF16)

    for k in range(KV_HEADS):
        if k % (KV_HEADS // 2) == 0:
            order = order_of(ids[2] ^ k)
        rows = [landed[i + k][...] for i in range(0, len(landed), KV_HEADS)]
        if run % 16:
            rows = [part.astype(F32) for part in rows]
        rows = jnp.concatenate([part.reshape(-1, width) for part in rows], axis=0).astype(BF16)
        laid = jnp.dot(order, rows, preferred_element_type=F32)
        request = ids[0] ^ turn(ids[2] ^ k)
        for u in range(run):
            laid_out[k, :, pl.ds(u * width, width)] = laid[u * blocks : (u + 1) * blocks].astype(BF16)
        copies.append(pltpu.make_async_copy(laid_out.at[k], out.at[0, 0, request], sems.at[1, k]))
        copies[-1].start()
    for copy in copies:
        copy.wait()


def shards(pool_kv, span_home, span_order, chosen, fresh_q, fresh_kv):
    pool_count, quads, heads = (lax.axis_size(a) for a in ("pool", "quad", "head"))
    seq_count = quads * heads
    me, quad, head = (lax.axis_index(a) for a in ("pool", "quad", "head"))
    slots, block, width = pool_kv.shape
    spans = span_order.shape[1]
    rows, q_width = fresh_q.shape[1:]
    kv_width = width // heads
    q_part = q_width // heads
    run = block // seq_count
    group = q_part // HEAD_DIM
    place = jnp.stack([me, quad, head, me ^ turn(head)]).astype(jnp.int32)
    ids = jnp.concatenate([place, span_home, span_order[0], chosen[0]])
    at_chosen = HOME + span_home.shape[0] + spans
    seat = quad * heads + head

    def after(value, *others):
        return lax.optimization_barrier((value, others))[0]

    def swap(value, axes, count, k):
        return lax.ppermute(value, axes, [(i, i ^ k) for i in range(count)])

    seq = ("quad", "head")
    to_pool = pl.pallas_call(
        functools.partial(pack_kernel, slots, spans),
        out_shape=[jax.ShapeDtypeStruct((block, kv_width), BF16)] * pool_count
        + [jax.ShapeDtypeStruct((block, width - kv_width), BF16)] * pool_count,
        in_specs=[SMEM, ANY],
        out_specs=[ANY] * (2 * pool_count),
        scratch_shapes=[pltpu.SemaphoreType.DMA((pool_count, heads))],
        compiler_params=PARAMS,
        cost_estimate=CHEAP,
        name="pack",
    )(ids, pool_kv)
    far = [swap(after(fresh_kv, to_pool[0]), "quad", quads, k) for k in range(1, quads)]

    def from_pool(values, out_shape, *dep):
        arrived = [values[0]] + [None] * (pool_count - 1)
        for k in reversed(range(1, pool_count)):
            arrived[k] = swap(values[k], "pool", pool_count, k)
        return pl.pallas_call(
            functools.partial(choose_kernel, slots, pool_count),
            out_shape=out_shape,
            in_specs=[SMEM] + [ANY] * pool_count,
            out_specs=[ANY] * len(out_shape),
            scratch_shapes=[pltpu.SemaphoreType.DMA((spans, heads - 1))],
            compiler_params=PARAMS,
            cost_estimate=CHEAP,
            name="choose",
        )(ids, *after(arrived, dep))

    blocks = jax.ShapeDtypeStruct((spans, block, kv_width), BF16)
    (own,) = from_pool(to_pool[:pool_count], [blocks], far)
    early = [swap(own, "quad", quads, a) for a in range(1, quads)]
    def place(got, send):
        like = jax.ShapeDtypeStruct(send.shape, BF16)
        return pl.pallas_call(
            place_kernel,
            out_shape=[jax.ShapeDtypeStruct(send.shape[1:], BF16), like],
            in_specs=[VMEM] * 2,
            out_specs=[VMEM] * 2,
            input_output_aliases={1: 1},
            compiler_params=PARAMS,
            cost_estimate=CHEAP,
            name="place",
        )(got, send)

    one = jax.ShapeDtypeStruct((rows, q_part + quads * kv_width), BF16)
    pair = jax.ShapeDtypeStruct((2, *one.shape), BF16)
    keep, give, send = pl.pallas_call(
        split_kernel,
        out_shape=[one, pair, pair],
        in_specs=[SMEM, ANY, ANY, ANY],
        out_specs=[ANY] * 3,
        scratch_shapes=[pltpu.SemaphoreType.DMA(((1 + quads) * heads,))],
        compiler_params=PARAMS,
        cost_estimate=CHEAP,
        name="split",
    )(ids, fresh_q, fresh_kv, far[0] if quads == 2 else jnp.concatenate(far, axis=0))
    chip = swap(send, "head", heads, 2)
    give = pl.pallas_call(
        follow_kernel,
        out_shape=pair,
        in_specs=[VMEM] * 2,
        out_specs=VMEM,
        input_output_aliases={1: 0},
        compiler_params=PARAMS,
        cost_estimate=CHEAP,
        name="follow",
    )(chip, give)
    core = swap(give, "head", heads, 1)
    q_give, q = give, [(keep, None), (core, 0), (chip, 0), (core, 1)]

    pair = jax.ShapeDtypeStruct((2, *blocks.shape), BF16)
    give, kv_send = from_pool(to_pool[pool_count:], [pair] * 2, send, early)
    beside, kv_send = place(after(swap(give, "head", heads, 1), q_give), kv_send)
    rest = swap(kv_send, "head", heads, 2)
    messages = [[(own, None)], [(beside, None)], [(rest, 0)], [(rest, 1)]]

    if rows % 16:
        q = [(jnp.concatenate([part if index is None else part[index] for part, index in q], axis=0), None)]
        listed = q[0][0][:, q_part:].reshape(heads, rows, quads, kv_width).transpose(2, 0, 1, 3)
        listed = listed.reshape(seq_count, rows, kv_width)
        fresh = jnp.take(listed, seat ^ jnp.arange(seq_count), axis=0).reshape(seq_count * rows, kv_width)
    else:
        arrays, views = arrays_of(q)
        fresh = pl.pallas_call(
            functools.partial(sort_kernel, quads, views),
            out_shape=jax.ShapeDtypeStruct((seq_count * rows, kv_width), BF16),
            in_specs=[SMEM] + [VMEM] * len(arrays),
            out_specs=VMEM,
            compiler_params=PARAMS,
            cost_estimate=CHEAP,
            name="sort",
        )(ids, *arrays)

    def to_decode(ks, *dep):
        parts = [messages[k] for k in ks]
        arrays, views = arrays_of([view for message in parts for view in message])
        arrays = after(arrays, dep)
        parts = group_views([(arrays[i], index) for i, index in views], parts)
        cut = cut_runs(ks, seq_count, run, heads, at_chosen, ids, fresh, parts)
        if run % 16:
            cut = [lax.dynamic_index_in_dim(jnp.stack(cut), head ^ k, axis=0, keepdims=False) for k in range(heads)]
        went = [None] * heads
        for k in reversed(range(heads)):
            perm = [
                ((r * quads + a) * heads + i, ((r ^ turn(i)) * quads + a) * heads + (i ^ k))
                for r in range(pool_count)
                for a in range(quads)
                for i in range(heads)
            ]
            went[k] = lax.ppermute(cut[k], ("pool", "quad", "head"), perm)
        return went, cut

    def work(ks, state, last=False):
        return attend(ks, state, last, seq_count, rows, group, at_chosen, ids, q, fresh, [messages[k] for k in ks])

    soons = []
    for a in range(1, quads):
        second = swap(beside, "quad", quads, a)
        messages += [[(early[a - 1], None)], [(second, None)], None, None]
    first = [0, 1, *range(heads, seq_count, heads)]
    state = None
    for at in range(0, len(first), 6):
        state = work(first[at : at + 6], state)
    firsts = [i for i in range(seq_count) if ahead(i)]
    for a in range(1, quads):
        at = a * heads
        soon = lax.ppermute(after(kv_send, fresh), ("quad", "head"), [(i, i ^ at ^ 2) for i in firsts])
        late = lax.ppermute(after(rest, messages[at + 1], state), ("quad", "head"), [(i, i ^ at) for i in firsts])
        messages[at + 2 : at + 4] = [[(soon, 0), (late, 0)], [(soon, 1), (late, 1)]]
        soons.append(soon)
    groups = [list(range(seq_count - 2)), [seq_count - 2, seq_count - 1]]
    second = [k for k in groups[0] if k not in first]
    landed = [to_decode(groups[0], state)]
    state = after(state, soons, landed[0][1])
    for at in range(0, len(second), 6):
        state = work(second[at : at + 6], state)
    keep, give, send = work(groups[-1], state, True)
    beside, send = place(swap(after(give, landed[0][0]), "head", heads, 1), send)
    landed.append(to_decode(groups[1], keep))
    chip = swap(send, "head", heads, 2)
    arrays, views = arrays_of([(keep, None), (beside, None), (chip, 0), (chip, 1)])
    runs = [part for went, _ in landed for part in went]
    return pl.pallas_call(
        functools.partial(finish_kernel, seq_count, views, len(arrays)),
        out_shape=[
            jax.ShapeDtypeStruct((1, rows, q_width), BF16),
            jax.ShapeDtypeStruct((1, 1, pool_count, spans * seq_count, run * kv_width), BF16),
        ],
        in_specs=[SMEM] + [VMEM] * (len(arrays) + len(runs)),
        out_specs=[ANY] * 2,
        scratch_shapes=[
            pltpu.VMEM((pool_count, spans * seq_count, run * kv_width), BF16),
            pltpu.SemaphoreType.DMA((2, max(pool_count, heads))),
        ],
        compiler_params=PARAMS,
        cost_estimate=CHEAP,
        name="finish",
    )(ids, *arrays, *runs)


def solution(mesh):
    pool_count, seq_count = mesh.shape["pool"], mesh.shape["seq"]
    fine = Mesh(mesh.devices.reshape(pool_count, seq_count // KV_HEADS, KV_HEADS), ("pool", "quad", "head"))
    seq = ("quad", "head")
    in_specs = (
        P("pool", seq, None),
        P(),
        P("pool", None),
        P("pool", None),
        P("pool", seq, None),
        P("pool", seq, None),
    )
    out_specs = (P("pool", seq, None), P("pool", seq, None, None, None))
    return jax.shard_map(shards, mesh=fine, in_specs=in_specs, out_specs=out_specs, check_vma=False)
```
